32 devices in a mesh: dp: 8 (over y, x, core), tensor: 4 (over z).
Axes of the slice: x: 2, y: 2, z: 4, core: 2. Of those that a mesh axis runs over, the one named last changes fastest.
Arguments:
- block_in: float32 [6304, 768], P(('dp', 'tensor')), may hold values from -6 to 6
- out_grad: float32 [6304, 768], P(('dp', 'tensor'))
- bank_w: float32 [4, 224, 64, 768], P('tensor', 'dp')
- bank_m: float32 [4, 224, 64, 768], P('tensor', 'dp')
- bank_v: float32 [4, 224, 64, 768], P('tensor', 'dp'), as said below
- norm_w: float32 [4, 768], replicated
- norm_m: float32 [4, 768], replicated
- norm_v: float32 [4, 768], replicated, as said below
- router_w: float32 [768, 4], replicated, may hold values from -0.14433756 to 0.14433756
- router_m: float32 [768, 4], replicated
- router_v: float32 [768, 4], replicated, as said below
- expert_ids: int32 [6304, 2], P('dp'), may hold values from 0 to 3, as said below
- fill_rank: int32 [6304, 2], P('dp'), may hold values from 0 to 1575, as said below
- owner_list: int32 [108], replicated, may hold values from 0 to 7, as said below
Outputs:
- block_out: float32 [6304, 768], P(('dp', 'tensor'))
- input_grad: float32 [6304, 768], P(('dp', 'tensor'))
- bank_first: float32 [4, 224, 64, 768], P('tensor', 'dp')
- bank_second: float32 [4, 224, 64, 768], P('tensor', 'dp')
- bank_new: float32 [4, 224, 64, 768], P('tensor', 'dp')
- norm_first: float32 [4, 768], replicated
- norm_second: float32 [4, 768], replicated
- norm_new: float32 [4, 768], replicated
- router_first: float32 [768, 4], replicated
- router_second: float32 [768, 4], replicated
- router_new: float32 [768, 4], replicated
The draws below stay inside these ranges and needn't reach their ends.
Inputs may be any that keep to these rules, and one draw needn't show every extreme that they name: `expert_ids`: the two entries of a row differ. `fill_rank`: within each group of 788 consecutive tokens the 1576 entries name every number of 0 to 1575 once. `owner_list`: no owner is named by more than 28 tiles, and some owner by exactly 28. `bank_v`: positive. `norm_v`: positive. `router_v`: positive.
All inputs are finite; a program needn't handle non-finite values.
Results may differ from the reference program's by a relative error of at most 0.02.
Values may be sent and summed in bfloat16 or wider, within the bound.
No kernel may reach another device: no remote copies, remote signals or barrier semaphores. Data moves between devices by JAX's collectives and lax.ppermute only.
A program may use at most 192 MiB of HBM per device.

```python
import jax
import jax.numpy as jnp
from jax import lax

D = 768
HEADS = 12
HEAD_DIM = 64
FF = 3072
SEQ = 197
EXPERTS = 4
STEP = 10
IMG = 4
GROUP_TOK = 788
TOKENS = 6304
CAPACITY = 443
TILES = 108
SLOTS = 28
BANK = 224
N_DP = 8
N_TENSOR = 4


def owner_draw(key):
    key = jax.random.fold_in(key, 11)
    first_key, second_key, third_key = jax.random.split(key, 3)
    full_owner = jax.random.randint(first_key, (), 0, N_DP).astype(jnp.int32)
    spread_slots = jax.random.permutation(second_key, (N_DP - 1) * SLOTS)[:TILES - SLOTS]
    other_owner = (spread_slots // SLOTS).astype(jnp.int32)
    other_owner = other_owner + (other_owner >= full_owner).astype(jnp.int32)
    listed = jnp.concatenate([jnp.zeros((SLOTS,), jnp.int32) + full_owner, other_owner])
    return listed[jax.random.permutation(third_key, TILES)].astype(jnp.int32)


def slot_kinds(key):
    owners_drawn = owner_draw(key)
    member = (owners_drawn[:, None] == jnp.arange(N_DP, dtype=jnp.int32)[None, :]).astype(jnp.int32)
    earlier = jnp.sum((jnp.cumsum(member, axis=0) - member) * member, axis=1)
    bank_spots = owners_drawn * SLOTS + earlier
    tile_number = jnp.arange(TILES, dtype=jnp.int32)
    heads_here = HEADS // N_TENSOR
    tile_runs = FF // (N_TENSOR * HEAD_DIM)
    tile_kind = jnp.where(tile_number < 3 * heads_here, 0, jnp.where(tile_number < 4 * heads_here, 1, 2 + (tile_number - 4 * heads_here) // tile_runs % 2))
    return jnp.full((BANK,), 4, jnp.int32).at[bank_spots].set(tile_kind.astype(jnp.int32))


def grad_table():
    return jnp.array([3.5, 1.0, 0.4, 0.2, 1.0], jnp.float32) * TOKENS ** 0.5


def draw_owner_list(key, part):
    listed = owner_draw(key)
    return listed


def draw_expert_ids(key, part):
    key = jax.random.fold_in(key, 17)
    level_key, favour_key, roll_key, first_key, second_key = jax.random.split(key, 5)
    group_count = TOKENS // GROUP_TOK
    levels = (jax.random.permutation(level_key, group_count) % 4).astype(jnp.int32)
    favoured = jax.random.randint(favour_key, (group_count,), 0, EXPERTS).astype(jnp.int32)
    token_group = (jnp.arange(TOKENS, dtype=jnp.int32) // GROUP_TOK).astype(jnp.int32)
    roll = jax.random.randint(roll_key, (TOKENS,), 0, 4096).astype(jnp.int32)
    drawn_first = jax.random.randint(first_key, (TOKENS,), 0, EXPERTS).astype(jnp.int32)
    first = jnp.where(roll < levels[token_group] * 700, favoured[token_group], drawn_first).astype(jnp.int32)
    step_on = jax.random.randint(second_key, (TOKENS,), 1, EXPERTS).astype(jnp.int32)
    second = ((first + step_on) % EXPERTS).astype(jnp.int32)
    return jnp.stack([first, second], axis=1).astype(jnp.int32)


def draw_fill_rank(key, part):
    key = jax.random.fold_in(key, 7)
    group_keys = jax.random.split(key, TOKENS // GROUP_TOK)
    ranks = jax.vmap(lambda group_key: jax.random.permutation(group_key, 2 * GROUP_TOK))(group_keys)
    return ranks.reshape(TOKENS, 2).astype(jnp.int32)


def draw_out_grad(key, part):
    key = jax.random.fold_in(key, 3)
    image_index = (jnp.arange(TOKENS, dtype=jnp.int32) // SEQ).astype(jnp.float32)
    image_total = TOKENS // SEQ
    rising = 1.0 + 2.0 * image_index / max(image_total - 1, 1)
    entries = jax.random.truncated_normal(key, -5.0, 5.0, (TOKENS, D), jnp.float32)
    return entries * rising[:, None]


def draw_bank_w(key, part):
    kinds_here = slot_kinds(key)
    key = jax.random.fold_in(key, 2)
    scale_table = jnp.array([1.3 * D ** (-0.5), 3.0 * D ** (-0.5), D ** (-0.5), 4.0 * FF ** (-0.5), D ** (-0.5)], jnp.float32)
    bank_shape = (N_TENSOR, BANK, HEAD_DIM, D)
    entries = jax.random.truncated_normal(key, -4.0, 4.0, bank_shape, jnp.float32)
    return entries * scale_table[kinds_here][None, :, None, None]


def draw_bank_m(key, part):
    kinds_here = slot_kinds(key)
    key = jax.random.fold_in(key, 4)
    bank_shape = (N_TENSOR, BANK, HEAD_DIM, D)
    entries = jax.random.truncated_normal(key, -4.0, 4.0, bank_shape, jnp.float32)
    return entries * (0.111 * grad_table()[kinds_here])[None, :, None, None]


def draw_bank_v(key, part):
    kinds_here = slot_kinds(key)
    key = jax.random.fold_in(key, 5)
    bank_shape = (N_TENSOR, BANK, HEAD_DIM, D)
    factor = jnp.exp(jax.random.uniform(key, bank_shape, jnp.float32, -0.693, 2.079))
    sizes_here = grad_table()[kinds_here]
    return factor * (0.0526 * sizes_here * sizes_here)[None, :, None, None]


def draw_norm_w(key, part):
    key = jax.random.fold_in(key, 6)
    entries = jax.random.truncated_normal(key, -4.0, 4.0, (4, D), jnp.float32)
    row_base = jnp.array([1.0, 0.0, 1.0, 0.0], jnp.float32)
    row_scale = jnp.array([0.1, 0.2, 0.1, 0.2], jnp.float32)
    return row_base[:, None] + row_scale[:, None] * entries


def norm_sizes():
    return jnp.array([6.0, 6.0, 1.0, 1.0], jnp.float32) * TOKENS ** 0.5


def draw_norm_m(key, part):
    key = jax.random.fold_in(key, 8)
    entries = jax.random.truncated_normal(key, -4.0, 4.0, (4, D), jnp.float32)
    return entries * (0.111 * norm_sizes())[:, None]


def draw_norm_v(key, part):
    key = jax.random.fold_in(key, 9)
    factor = jnp.exp(jax.random.uniform(key, (4, D), jnp.float32, -0.693, 2.079))
    sizes_here = norm_sizes()
    return factor * (0.0526 * sizes_here * sizes_here)[:, None]


def draw_router_m(key, part):
    key = jax.random.fold_in(key, 12)
    router_size = 30.0 * TOKENS ** 0.5
    entries = jax.random.truncated_normal(key, -4.0, 4.0, (D, EXPERTS), jnp.float32)
    return entries * (0.111 * router_size)


def draw_router_v(key, part):
    key = jax.random.fold_in(key, 13)
    router_size = 30.0 * TOKENS ** 0.5
    factor = jnp.exp(jax.random.uniform(key, (D, EXPERTS), jnp.float32, -0.693, 2.079))
    return factor * (0.0526 * router_size * router_size)


def block_scale(key, shape, pieces, low, top_value):
    def one(dim, blocks):
        steps = jax.random.uniform(jax.random.fold_in(jax.random.fold_in(key, 6), dim), (blocks,), jnp.float32, low / len(pieces), top_value / len(pieces))
        return jnp.repeat(jnp.exp(steps), shape[dim] // blocks).reshape((-1,) + (1,) * (len(shape) - dim - 1))

    gain = one(*pieces[0])
    for cut in pieces[1:]:
        gain = gain * one(*cut)
    return gain


def gaussian(rng, shape, spread, reach, pieces=(), kind=jnp.bfloat16):
    values = spread * jax.random.normal(rng, shape, jnp.float32)
    if pieces:
        values = values * block_scale(rng, shape, pieces, -0.22, 0.18)
    return jnp.clip(values, -reach, reach).astype(kind)


def setup_inputs(seed: int = 0) -> dict:
    splits = jax.random.split(jax.random.key(seed), 15)
    return {
        "block_in": gaussian(splits[0], (TOKENS, D), 1.0, 6.0, ((0, 32),), jnp.float32),
        "out_grad": draw_out_grad(jax.random.fold_in(splits[14], 71), 0),
        "bank_w": draw_bank_w(jax.random.fold_in(splits[14], 71), 0),
        "bank_m": draw_bank_m(jax.random.fold_in(splits[14], 71), 0),
        "bank_v": draw_bank_v(jax.random.fold_in(splits[14], 71), 0),
        "norm_w": draw_norm_w(jax.random.fold_in(splits[14], 71), 0),
        "norm_m": draw_norm_m(jax.random.fold_in(splits[14], 71), 0),
        "norm_v": draw_norm_v(jax.random.fold_in(splits[14], 71), 0),
        "router_w": gaussian(splits[8], (D, EXPERTS), (0.8 * D ** -0.5), 0.14433756, (), jnp.float32),
        "router_m": draw_router_m(jax.random.fold_in(splits[14], 71), 0),
        "router_v": draw_router_v(jax.random.fold_in(splits[14], 71), 0),
        "expert_ids": draw_expert_ids(jax.random.fold_in(splits[14], 71), 0),
        "fill_rank": draw_fill_rank(jax.random.fold_in(splits[14], 71), 0),
        "owner_list": draw_owner_list(jax.random.fold_in(splits[14], 71), 0),
    }


@jax.custom_vjp
def low(v):
    return lax.optimization_barrier(v.astype(jnp.bfloat16)).astype(jnp.float32)

@jax.custom_vjp
def low_back(v):
    return v

def low_keep(v):
    return (low(v), None)

def low_pass(kept, grad):
    return (grad,)

def back_keep(v):
    return (v, None)

def back_low(kept, grad):
    return (low(grad),)
low.defvjp(low_keep, low_pass)
low_back.defvjp(back_keep, back_low)
norm_epsilon = 1e-06
beta_first = 0.9
beta_second = 0.95
adam_epsilon = 1e-08
weight_decay = 0.1
rate_bank = 0.06
rate_norm = 0.25
rate_router = 0.05
highest = lax.Precision.HIGHEST

def layer_norm(values, gain_row, bias_row):
    center = values - lax.optimization_barrier(jnp.mean(values, axis=-1, keepdims=True))
    variance = lax.optimization_barrier(jnp.mean(center * center, axis=-1, keepdims=True))
    return center * lax.rsqrt(variance + norm_epsilon) * gain_row + bias_row

def adamw_update(weights, first_old, second_old, grad_total, step_rate, decay_rate):
    first_new = beta_first * first_old + (1.0 - beta_first) * grad_total
    second_new = beta_second * second_old + (1.0 - beta_second) * grad_total * grad_total
    first_hat = first_new / (1.0 - beta_first ** STEP)
    second_hat = second_new / (1.0 - beta_second ** STEP)
    weights_new = weights * (1.0 - step_rate * decay_rate) - step_rate * first_hat / (jnp.sqrt(second_hat) + adam_epsilon)
    return (first_new, second_new, weights_new)

def bank_positions(owner_list):
    owners = jnp.arange(N_DP, dtype=jnp.int32)
    member = (owner_list[:, None] == owners[None, :]).astype(jnp.int32)
    earlier = lax.optimization_barrier(jnp.sum((jnp.cumsum(member, axis=0) - member) * member, axis=1))
    return (owner_list * SLOTS + earlier).astype(jnp.int32)

def slot_table(expert_ids, fill_rank):
    pair_count = 2 * GROUP_TOK
    pair_expert = expert_ids.reshape(pair_count).astype(jnp.int32)
    pair_rank = fill_rank.reshape(pair_count).astype(jnp.int32)
    pair_number = jnp.arange(pair_count, dtype=jnp.int32)
    by_rank = jnp.zeros((pair_count,), jnp.int32).at[pair_rank].set(pair_number)
    ranked_expert = pair_expert[by_rank]
    member = (ranked_expert[:, None] == jnp.arange(EXPERTS, dtype=jnp.int32)[None, :]).astype(jnp.int32)
    earlier = lax.optimization_barrier(jnp.sum((jnp.cumsum(member, axis=0) - member) * member, axis=1))
    placed = earlier[pair_rank]
    slot_count = EXPERTS * CAPACITY
    pair_slot = jnp.where(placed < CAPACITY, pair_expert * CAPACITY + placed, slot_count).astype(jnp.int32)
    slot_token = jnp.full((slot_count + 1,), GROUP_TOK, jnp.int32).at[pair_slot].set(pair_number // 2)
    return (pair_slot.reshape(GROUP_TOK, 2), slot_token[:slot_count])

def group_layer(block_rows, weight_tiles, norm_rows, router_low, expert_ids, pair_slot, slot_token):
    heads_here = HEADS // N_TENSOR
    tile_runs = FF // (N_TENSOR * HEAD_DIM)
    model_heads = HEADS * HEAD_DIM
    qkv_tiles = weight_tiles[:, :3 * heads_here].reshape(N_TENSOR, 3, heads_here, HEAD_DIM, D)
    proj_in = jnp.transpose(qkv_tiles, (1, 0, 2, 3, 4)).reshape(3 * model_heads, D)
    proj_out = weight_tiles[:, 3 * heads_here:4 * heads_here].reshape(model_heads, D)
    expert_tiles = weight_tiles[:, 4 * heads_here:].reshape(N_TENSOR, EXPERTS, 2, tile_runs, HEAD_DIM, D)
    expert_in = jnp.transpose(expert_tiles[:, :, 0], (1, 0, 2, 3, 4)).reshape(EXPERTS, FF, D)
    expert_out = jnp.transpose(expert_tiles[:, :, 1], (1, 0, 2, 3, 4)).reshape(EXPERTS, FF, D)
    normed = low(layer_norm(block_rows, norm_rows[0], norm_rows[1]))
    mixed = low(low_back(jnp.dot(normed, proj_in.T, precision=highest)))
    mixed = mixed.reshape(IMG, SEQ, 3, HEADS, HEAD_DIM)
    queries = mixed[:, :, 0]
    key_heads = mixed[:, :, 1]
    value_heads = mixed[:, :, 2]
    scores = low_back(jnp.einsum('bqhd,bkhd->bhqk', queries, key_heads, precision=highest) * HEAD_DIM ** (-0.5))
    attn_probs = low(jax.nn.softmax(scores, axis=-1))
    attended = low(low_back(jnp.einsum('bhqk,bkhd->bqhd', attn_probs, value_heads, precision=highest)))
    branch = low_back(jnp.dot(attended.reshape(GROUP_TOK, model_heads), proj_out, precision=highest))
    residual = block_rows + branch
    second = low(layer_norm(residual, norm_rows[2], norm_rows[3]))
    router_probs = jax.nn.softmax(jnp.dot(second, router_low, precision=highest), axis=-1)
    gate_pair = jnp.take_along_axis(router_probs, expert_ids, axis=1)
    second_pad = jnp.concatenate([second, jnp.zeros((1, D), jnp.float32)], axis=0)
    dispatched = second_pad[slot_token].reshape(EXPERTS, CAPACITY, D)
    hidden = low_back(jnp.einsum('ecd,efd->ecf', dispatched, expert_in, precision=highest))
    activated = low(jax.nn.gelu(hidden))
    returned = low_back(jnp.einsum('ecf,efd->ecd', activated, expert_out, precision=highest))
    flat_out = jnp.concatenate([returned.reshape(EXPERTS * CAPACITY, D), jnp.zeros((1, D), jnp.float32)], axis=0)
    combined = low_back(lax.optimization_barrier(jnp.sum(gate_pair[:, :, None] * flat_out[pair_slot], axis=1)))
    return residual + combined

def whole_layer(block_in, bank_w, norm_w, router_w, expert_ids, pair_slots, slot_tokens, positions):
    weight_tiles = low(bank_w)[:, positions]
    router_low = low(router_w)

    def one_group(carry_value, group_data):
        rows, ids_group, slots_group, tokens_group = group_data
        return (carry_value, group_layer(rows, weight_tiles, norm_w, router_low, ids_group, slots_group, tokens_group))
    blocks = (block_in.reshape(N_DP, GROUP_TOK, D), expert_ids.reshape(N_DP, GROUP_TOK, 2), pair_slots, slot_tokens)
    _, outputs = lax.scan(jax.checkpoint(one_group), jnp.zeros((), jnp.float32), blocks)
    return outputs.reshape(TOKENS, D)

def reference(block_in, out_grad, bank_w, bank_m, bank_v, norm_w, norm_m, norm_v, router_w, router_m, router_v, expert_ids, fill_rank, owner_list):
    positions = bank_positions(owner_list)
    pair_slots, slot_tokens = lax.map(lambda group_pair: slot_table(group_pair[0], group_pair[1]), (expert_ids.reshape(N_DP, GROUP_TOK, 2), fill_rank.reshape(N_DP, GROUP_TOK, 2)))

    def layer_call(block_values, bank_values, norm_values, router_values):
        return whole_layer(block_values, bank_values, norm_values, router_values, expert_ids, pair_slots, slot_tokens, positions)
    block_out, pullback = jax.vjp(layer_call, block_in, bank_w, norm_w, router_w)
    input_grad, bank_grad, norm_grad, router_grad = pullback(out_grad)
    bank_first, bank_second, bank_new = adamw_update(bank_w, bank_m, bank_v, bank_grad, rate_bank, weight_decay)
    norm_first, norm_second, norm_new = adamw_update(norm_w, norm_m, norm_v, norm_grad, rate_norm, 0.0)
    router_first, router_second, router_new = adamw_update(router_w, router_m, router_v, router_grad, rate_router, weight_decay)
    return (block_out, input_grad, bank_first, bank_second, bank_new, norm_first, norm_second, norm_new, router_first, router_second, router_new)
```

```python
import functools

import jax
import jax.numpy as jnp
from jax import lax
from jax.experimental import pallas as pl
from jax.experimental.pallas import tpu as pltpu
from jax.sharding import PartitionSpec as P

HEADS = 12
FF = 3072
SEQ = 197
EXPERTS = 4
STEP = 10
CAPACITY = 443

ROWS = -(-SEQ // 16) * 16
SLOTS = -(-CAPACITY // 16) * 16
ROUTER_ROWS = 16
VMEM_BYTES = 56 * 1024 * 1024

norm_epsilon = 1e-06
beta_first = 0.9
beta_second = 0.95
adam_epsilon = 1e-08
weight_decay = 0.1
rate_bank = 0.06
rate_norm = 0.25
rate_router = 0.05
highest = lax.Precision.HIGHEST
low_type = jnp.bfloat16
full_type = jnp.float32


def dot_nn(left, right):
    return lax.dot_general(left, right, (((1,), (0,)), ((), ())), preferred_element_type=full_type)


def dot_nt(left, right):
    return lax.dot_general(left, right, (((1,), (1,)), ((), ())), preferred_element_type=full_type)


def dot_tn(left, right):
    return lax.dot_general(left, right, (((0,), (0,)), ((), ())), preferred_element_type=full_type)


def adamw_update(weights, first_old, second_old, grad_total, step_rate, decay_rate):
    first_new = beta_first * first_old + (1.0 - beta_first) * grad_total
    second_new = beta_second * second_old + (1.0 - beta_second) * grad_total * grad_total
    first_scale = step_rate / (1.0 - beta_first**STEP)
    second_scale = 1.0 / (1.0 - beta_second**STEP)
    weights_new = weights * (1.0 - step_rate * decay_rate) - first_new * first_scale / (
        jnp.sqrt(second_new * second_scale) + adam_epsilon
    )
    return (first_new, second_new, weights_new)


def call(body, grid, in_specs, out_specs, out_shape, scratch=(), prefetch=0, flops=0, moved=0):
    return pl.pallas_call(
        body,
        grid_spec=pltpu.PrefetchScalarGridSpec(
            num_scalar_prefetch=prefetch,
            grid=grid,
            in_specs=in_specs,
            out_specs=out_specs,
            scratch_shapes=list(scratch),
        ),
        out_shape=out_shape,
        compiler_params=pltpu.CompilerParams(vmem_limit_bytes=VMEM_BYTES),
        cost_estimate=pl.CostEstimate(flops=flops, bytes_accessed=moved, transcendentals=0),
    )


def whole(shape):
    return pl.BlockSpec(shape, lambda *_: (0,) * len(shape))


def shaped(shape, kind):
    return jax.ShapeDtypeStruct(shape, kind)


def row_mask(rows):
    return lax.broadcasted_iota(jnp.int32, (rows, 1), 0) < SEQ


def normalize(values):
    center = values - jnp.mean(values, axis=-1, keepdims=True)
    variance = jnp.mean(center * center, axis=-1, keepdims=True)
    spread = lax.rsqrt(variance + norm_epsilon)
    return center * spread, spread


def norm_back(scaled, spread, grad_rows, gain_row):
    inner = grad_rows * gain_row
    mean_one = jnp.mean(inner, axis=-1, keepdims=True)
    mean_two = jnp.mean(inner * scaled, axis=-1, keepdims=True)
    return spread * (inner - mean_one - scaled * mean_two)


def first_kernel(block_ref, grad_ref, out_ref):
    mask = row_mask(ROWS)
    model = block_ref.shape[1]
    scaled, _ = normalize(jnp.where(mask, block_ref[...], 0.0))
    out_ref[:, :model] = jnp.where(mask, scaled, 0.0).astype(low_type)
    out_ref[:, model:] = jnp.where(mask, grad_ref[...], 0.0).astype(low_type)


def dispatch_kernel(pair_count, col_ref, row_ref, pick_ref, place_ref, slot_row, slot_col):
    expert = pl.program_id(0)
    tokens = row_ref.shape[1]
    chunk = ROWS // 2

    @pl.when(expert == 0)
    def _():
        row_zero = row_ref[0:1, :]
        row_one = row_ref[1:2, :]

        def ones(condition):
            return jnp.where(condition, 1.0, 0.0)

        bounds = [float(e * pair_count) for e in range(1, EXPERTS)]
        below = [
            jnp.sum(ones(row_zero < b) + ones(row_one < b), axis=1, keepdims=True) for b in bounds
        ]

        def slots(keys, lower):
            base = jnp.zeros_like(keys)
            index = jnp.zeros_like(keys)
            for bound, count in zip(bounds, below):
                base = jnp.where(keys >= bound, jnp.broadcast_to(count, keys.shape), base)
                index = index + ones(keys >= bound)
            placed = lower - base
            kept = jnp.logical_and(placed < CAPACITY, keys < float(EXPERTS * pair_count))
            return jnp.where(kept, index * SLOTS + placed, -1.0)

        def step(i, carried):
            low_zero, low_one = carried
            start = pl.multiple_of(i * chunk, 8)
            keys = col_ref[pl.ds(start, chunk), :]
            zero = keys[:, 0:1]
            one = keys[:, 1:2]
            before_zero = jnp.sum(
                ones(row_zero < zero) + ones(row_one < zero), axis=1, keepdims=True
            )
            before_one = jnp.sum(ones(row_zero < one) + ones(row_one < one), axis=1, keepdims=True)
            slot_col[pl.ds(start, chunk), 0:1] = slots(zero, before_zero)
            slot_col[pl.ds(start, chunk), 1:2] = slots(one, before_one)
            low_zero = low_zero + jnp.sum(
                ones(zero < row_zero) + ones(one < row_zero), axis=0, keepdims=True
            )
            low_one = low_one + jnp.sum(
                ones(zero < row_one) + ones(one < row_one), axis=0, keepdims=True
            )
            return low_zero, low_one

        nothing = jnp.zeros((1, tokens), full_type)
        low_zero, low_one = lax.fori_loop(0, tokens // chunk, step, (nothing, nothing))
        slot_row[0:1, :] = slots(row_zero, low_zero)
        slot_row[1:2, :] = slots(row_one, low_one)

    begin = expert * SLOTS
    down = (lax.broadcasted_iota(jnp.int32, (SLOTS, 1), 0) + begin).astype(full_type)
    hit = jnp.logical_or(slot_row[0:1, :] == down, slot_row[1:2, :] == down)
    pick_ref[0] = jnp.where(hit, 1.0, 0.0).astype(low_type)

    @pl.when(expert == 0)
    def _():
        across = lax.broadcasted_iota(jnp.int32, (1, EXPERTS * SLOTS), 1).astype(full_type)
        hit = jnp.logical_or(slot_col[:, 0:1] == across, slot_col[:, 1:2] == across)
        place_ref[...] = jnp.where(hit, 1.0, 0.0).astype(low_type)


def fetch_tiles(table_ref, pieces, first, last, start, offset=0):
    for piece in pieces:

        def step(j, carried, piece=piece, offset=offset):
            tile = table_ref[offset + j]

            @pl.when(jnp.logical_and(tile >= first, tile < last))
            def _():
                start(piece.at[j], tile)

            return carried

        lax.fori_loop(0, piece.shape[0], step, 0)
        offset += piece.shape[0]


def softmax_rows(scores):
    valid = lax.broadcasted_iota(jnp.int32, scores.shape, 1) < SEQ
    scores = jnp.where(valid, scores, -1e30)
    top = jnp.max(scores, axis=-1, keepdims=True)
    powers = jnp.exp(scores - top)
    return powers / jnp.sum(powers, axis=-1, keepdims=True)


def attend_kernel(heads, banks, table_ref, *refs):
    bank, refs = refs[:banks], refs[banks:]
    scaled_ref, norm_ref = refs[:2]
    normed_ref, mixed_ref, attended_ref, branch_ref, tiles, semaphore = refs[-6:]
    count, head, model = tiles.shape

    @pl.when(pl.program_id(0) == 0)
    def _():
        def start(source, tile):
            pltpu.make_async_copy(source, tiles.at[tile], semaphore).start()

        fetch_tiles(table_ref, bank, 0, count, start)
        pltpu.make_async_copy(tiles, tiles, semaphore).wait()

    width = heads * head
    proj_in = tiles[: 3 * heads].reshape(3 * width, model)
    proj_out = tiles[3 * heads :].reshape(width, model)
    mask = row_mask(ROWS)
    rows = scaled_ref[...].astype(full_type) * norm_ref[0:1, :] + norm_ref[1:2, :]
    rows = jnp.where(mask, rows, 0.0).astype(low_type)
    normed_ref[...] = rows
    mixed = dot_nt(rows, proj_in).astype(low_type)
    mixed_ref[0] = mixed
    parts = []
    for h in range(heads):
        query, key, value = (
            mixed[:, p * width + h * head : p * width + (h + 1) * head] for p in range(3)
        )
        probs = softmax_rows(dot_nt(query, key) * head**-0.5).astype(low_type)
        parts.append(dot_nn(probs, value))
    attended = jnp.where(mask, jnp.concatenate(parts, axis=1), 0.0).astype(low_type)
    attended_ref[0] = attended
    branch_ref[...] = dot_nn(attended, proj_out).astype(low_type)


def second_kernel(block_ref, norm_ref, branch_ref, residual_ref, second_ref):
    mask = row_mask(ROWS)
    residual = jnp.where(mask, block_ref[...], 0.0) + branch_ref[...].astype(full_type)
    residual_ref[...] = residual
    scaled, _ = normalize(residual)
    rows = scaled * norm_ref[2:3, :] + norm_ref[3:4, :]
    second_ref[...] = jnp.where(mask, rows, 0.0).astype(low_type)


def gelu_pair(values):
    factor = 0.7978845608028654
    square = values * values
    bent = jnp.tanh(factor * values * (1.0 + 0.044715 * square))
    half = 0.5 * (1.0 + bent)
    slope = half + 0.5 * factor * values * (1.0 - bent * bent) * (1.0 + 0.134145 * square)
    return values * half, slope


def expert_probs(router_rows, second_rows):
    logits = dot_nt(router_rows, second_rows)
    real = lax.broadcasted_iota(jnp.int32, logits.shape, 0) < EXPERTS
    logits = jnp.where(real, logits, -1e30)
    powers = jnp.exp(logits - jnp.max(logits, axis=0, keepdims=True))
    return powers / jnp.sum(powers, axis=0, keepdims=True)


def pick_kernel(cotangent_ref, pick_ref, _, rows_ref):
    rows_ref[0] = dot_nn(pick_ref[0], cotangent_ref[...]).astype(low_type)


def prepare_kernel(base, banks, table_ref, *refs):
    bank, refs = refs[:banks], refs[banks:]
    tiles_ref, semaphore = refs[-2:]
    count = tiles_ref.shape[0]

    def start(source, tile):
        pltpu.make_async_copy(source, tiles_ref.at[tile - base], semaphore).start()

    fetch_tiles(table_ref, bank, base, base + count, start)
    pltpu.make_async_copy(tiles_ref, tiles_ref, semaphore).wait()


def expert_kernel(images, runs, place_of_ref, *refs):
    tiles_ref, grads_ref, second_ref, router_ref, pick_ref, place_ref = refs[:6]
    first_ref, sent_ref, kept_ref, gated_ref, piece_ref = refs[6:11]
    probs, pair_grad, rows_back, place, stage, out_semaphore, place_semaphore = refs[11:]
    expert = pl.program_id(0)
    model = second_ref.shape[1]
    hidden_width = runs * tiles_ref.shape[2]
    place_copy = pltpu.make_async_copy(place_ref, place, place_semaphore)

    @pl.when(expert == 0)
    def _():
        place_copy.start()
        probs[...] = expert_probs(router_ref[...], second_ref[...])
        pair_grad[...] = jnp.zeros_like(pair_grad)

    weight_in = tiles_ref[0, :runs].reshape(hidden_width, model)
    weight_out = tiles_ref[0, runs:].reshape(hidden_width, model)
    pick = pick_ref[0]
    pick_full = pick.astype(full_type)
    gate = jnp.sum(pick_full * probs[pl.ds(expert, 1), :], axis=1, keepdims=True)
    grad_rows = grads_ref[0].astype(full_type)
    back = (gate * grad_rows).astype(low_type)
    rows = dot_nn(pick, second_ref[...]).astype(low_type)
    hidden = dot_nt(rows, weight_in)
    act_grad = dot_nt(back, weight_out)
    activated, slope = gelu_pair(hidden)
    activated = activated.astype(low_type)
    hidden_grad = (act_grad * slope).astype(low_type)
    returned = dot_nn(activated, weight_out)
    here = pl.ds(pl.multiple_of(expert * SLOTS, SLOTS), SLOTS)
    rows_back[here, :] = dot_nn(hidden_grad, weight_in).astype(low_type)
    gate_grad = jnp.sum(grad_rows * returned, axis=1, keepdims=True)
    pair_grad[pl.ds(expert, 1), :] = jnp.sum(pick_full * gate_grad, axis=0, keepdims=True)
    gated_ref[0] = (gate * returned).astype(low_type)
    slot = lax.rem(expert, 2)
    sent_count = 1 + sent_ref.shape[0]

    def settle(which, m):
        copy = stage.at[which, m]
        pltpu.make_async_copy(copy, copy, out_semaphore.at[which, m]).wait()

    for m, (left, right) in enumerate(((hidden_grad, rows), (activated, back))):

        @pl.when(expert >= 2)
        def _(m=m):
            settle(slot, m)

        stage[slot, m] = dot_tn(left, right).astype(low_type).reshape(stage.shape[2:])
        target = place_of_ref[2 * expert + m]
        copy = (stage.at[slot, m], out_semaphore.at[slot, m])

        @pl.when(target == 0)
        def _(copy=copy):
            pltpu.make_async_copy(copy[0], first_ref, copy[1]).start()

        @pl.when(jnp.logical_and(target > 0, target < sent_count))
        def _(target=target, copy=copy):
            pltpu.make_async_copy(copy[0], sent_ref.at[target - 1], copy[1]).start()

        @pl.when(target >= sent_count)
        def _(target=target, copy=copy):
            pltpu.make_async_copy(copy[0], kept_ref.at[target - sent_count], copy[1]).start()

    @pl.when(expert == EXPERTS - 1)
    def _():
        place_copy.wait()
        total = dot_nn(place[...], rows_back[...])
        for s in range(images):
            first = s * (ROWS + ROUTER_ROWS)
            last = first + ROWS + ROUTER_ROWS
            middle = first + ROWS
            here = slice(s * ROWS, (s + 1) * ROWS)
            piece_ref[first:middle, :] = total[here, :].astype(low_type)
            piece_ref[middle:last, :] = jnp.zeros((ROUTER_ROWS, model), low_type)
            piece_ref[middle:last, :ROWS] = pair_grad[:, here].astype(low_type)
        for which in range(2):
            for m in range(2):
                settle(which, m)


def combine_kernel(gated_ref, place_ref, out_ref):
    out_ref[...] = dot_nn(place_ref[...], gated_ref[...]).astype(low_type)


def second_back_kernel(
    residual_ref, grad_ref, second_ref, router_ref, norm_ref, piece_ref, *refs
):
    rows_ref, low_ref, small_ref = refs[-3:]
    mask = row_mask(ROWS)
    total = piece_ref[...].astype(full_type)
    second = second_ref[...]
    router_rows = router_ref[...]
    probs = expert_probs(router_rows, second)
    probs_grad = total[ROWS:, :ROWS]
    logit_grad = probs * (probs_grad - jnp.sum(probs * probs_grad, axis=0, keepdims=True))
    second_grad = total[:ROWS, :] + lax.dot_general(
        logit_grad,
        router_rows.astype(full_type),
        (((0,), (0,)), ((), ())),
        precision=highest,
        preferred_element_type=full_type,
    )
    router_grad = lax.dot_general(
        logit_grad,
        second.astype(full_type),
        (((1,), (0,)), ((), ())),
        precision=highest,
        preferred_element_type=full_type,
    )
    second_grad = jnp.where(mask, second_grad, 0.0)
    scaled, spread = normalize(residual_ref[...])
    part = norm_back(scaled, spread, second_grad, norm_ref[2:3, :])
    rows = jnp.where(mask, grad_ref[...] + part, 0.0)
    rows_ref[...] = rows
    low_ref[...] = rows.astype(low_type)
    small_ref[0:1, :] = jnp.sum(second_grad * scaled, axis=0, keepdims=True)
    small_ref[1:2, :] = jnp.sum(second_grad, axis=0, keepdims=True)
    small_ref[2 : 2 + EXPERTS, :] = router_grad[:EXPERTS, :]
    small_ref[2 + EXPERTS :, :] = jnp.zeros((6 - EXPERTS, small_ref.shape[1]), full_type)


def attend_back_kernel(images, heads, banks, table_ref, core_ref, *refs):
    bank, refs = refs[:banks], refs[banks:]
    (
        branch_ref,
        scaled_ref,
        normed_ref,
        mixed_ref,
        attended_ref,
        small_two_ref,
        own_ref,
        other_ref,
        piece_ref,
        small_ref,
        tiles,
        cotangent,
        normed,
        mixed_grad,
        attended,
        semaphore,
    ) = refs
    count, head, model = tiles.shape
    image = pl.program_id(0)

    @pl.when(image == 0)
    def _():
        def start(source, tile):
            pltpu.make_async_copy(source, tiles.at[tile], semaphore).start()

        fetch_tiles(table_ref, bank, 0, count, start)
        pltpu.make_async_copy(tiles, tiles, semaphore).wait()
        small_ref[0:2, :] = jnp.zeros((2, model), full_type)
        small_ref[2:, :] = small_two_ref[:6, :]

    width = heads * head
    scale = head**-0.5
    proj_in = tiles[: 3 * heads].reshape(3 * width, model)
    proj_out = tiles[3 * heads :].reshape(width, model)
    here = pl.ds(pl.multiple_of(image * ROWS, ROWS), ROWS)
    branch = branch_ref[...]
    cotangent[here, :] = branch
    normed[here, :] = normed_ref[...]
    attended[here, :] = attended_ref[0]
    attended_grad = dot_nt(branch, proj_out).astype(low_type)
    mixed = mixed_ref[0]
    parts = [[], [], []]
    for h in range(heads):
        query, key, value = (
            mixed[:, p * width + h * head : p * width + (h + 1) * head] for p in range(3)
        )
        above = attended_grad[:, h * head : (h + 1) * head]
        probs = softmax_rows(dot_nt(query, key) * scale)
        weight_grad = dot_nt(above, value)
        inner = jnp.sum(probs * weight_grad, axis=-1, keepdims=True)
        score_grad = (probs * (weight_grad - inner)).astype(low_type)
        parts[0].append(dot_nn(score_grad, key) * scale)
        parts[1].append(dot_tn(score_grad, query) * scale)
        parts[2].append(dot_tn(probs.astype(low_type), above))
    grads = jnp.concatenate(parts[0] + parts[1] + parts[2], axis=1).astype(low_type)
    mixed_grad[here, :] = grads
    back = dot_nn(grads, proj_in)
    piece_ref[...] = back.astype(low_type)
    small_ref[0:1, :] += jnp.sum(back * scaled_ref[...].astype(full_type), axis=0, keepdims=True)
    small_ref[1:2, :] += jnp.sum(back, axis=0, keepdims=True)

    @pl.when(image == images - 1)
    def _():
        tile_grads = jnp.concatenate(
            [
                dot_tn(mixed_grad[...], normed[...]).astype(low_type),
                dot_tn(attended[...], cotangent[...]).astype(low_type),
            ],
            axis=0,
        )
        rows = count // 2 * head
        rest = tile_grads.reshape(2, rows, model)

        @pl.when(core_ref[0] == 0)
        def _():
            own_ref[:rows, :] = rest[0]
            other_ref[:rows, :] = rest[1]

        @pl.when(core_ref[0] == 1)
        def _():
            own_ref[:rows, :] = rest[1]
            other_ref[:rows, :] = rest[0]

        for ref in (own_ref, other_ref):
            ref[rows:, :] = split_sums(small_ref[...])


def split_sums(rows):
    high = rows.astype(low_type)
    low = (rows - high.astype(full_type)).astype(low_type)
    return jnp.concatenate([high.astype(full_type), low.astype(full_type)], axis=0).astype(low_type)


def join_sums(rows):
    wide = rows.astype(full_type)
    return wide[:8, :] + wide[8:, :]


def near_add_kernel(count, left_ref, right_ref, *refs):
    outs = refs[-count:]
    rows = left_ref.shape[0] - 16
    total = left_ref[:rows, :].astype(full_type) + right_ref[:rows, :].astype(full_type)
    sums = split_sums(join_sums(left_ref[rows:, :]) + join_sums(right_ref[rows:, :]))
    outs[0][:rows, :] = total.astype(low_type)
    outs[-1][outs[-1].shape[0] - 16 :, :] = sums


def last_sum_kernel(images, here_ref, *refs):
    pieces, out_ref, held = refs[:images], refs[-2], refs[-1]
    for s in range(images):
        held[lax.rem(here_ref[0] + s, images)] = join_sums(pieces[s][...])
    total = held[0]
    for s in range(1, images):
        total = total + held[s]
    out_ref[...] = total


def first_back_kernel(block_ref, grad_ref, norm_ref, residual_ref, piece_ref, added_ref, *refs):
    grad_out, block_out = refs[-2:]
    mask = row_mask(ROWS)
    total = jnp.where(mask, piece_ref[...].astype(full_type), 0.0)
    scaled, spread = normalize(jnp.where(mask, block_ref[...], 0.0))
    grad_out[...] = grad_ref[...] + norm_back(scaled, spread, total, norm_ref[0:1, :])
    block_out[...] = residual_ref[...] + added_ref[...].astype(full_type)


def bank_kernel(pieces, plan_ref, *refs):
    olds = refs[:3]
    sources = refs[3 : 3 + pieces]
    outs = refs[-9:-6]
    held, fresh, grads, held_semaphore, fresh_semaphore, grad_semaphore = refs[-6:]
    ahead, behind, width = held.shape[0], fresh.shape[0], grads.shape[0]
    count = plan_ref[2 * width]

    def load(j):
        slot, row = plan_ref[j], lax.rem(j, ahead)
        for k in range(3):
            pltpu.make_async_copy(
                olds[k].at[0, slot], held.at[row, k], held_semaphore.at[row, k]
            ).start()

    def settle(ref, semaphore):
        pltpu.make_async_copy(ref, ref, semaphore).wait()

    for j in range(ahead - 1):
        pl.when(j < count)(functools.partial(load, j))

    def start(source, slot):
        pltpu.make_async_copy(source, grads.at[slot], grad_semaphore.at[slot]).start()

    fetch_tiles(plan_ref, sources, 0, width, start, 2 * width + 1)

    def step(j, carried):
        pl.when(j + ahead - 1 < count)(lambda: load(j + ahead - 1))
        slot, row, out_row = plan_ref[j], lax.rem(j, ahead), lax.rem(j, behind)
        used = plan_ref[width + slot]
        for k in range(3):
            settle(held.at[row, k], held_semaphore.at[row, k])
        pl.when(used == 1)(lambda: settle(grads.at[slot], grad_semaphore.at[slot]))
        grad = jnp.where(used == 1, grads[slot].astype(full_type), 0.0)
        updated = adamw_update(*(held[row, k] for k in range(3)), grad, rate_bank, weight_decay)
        for k, value in enumerate(updated):
            pl.when(j >= behind)(
                lambda k=k: settle(fresh.at[out_row, k], fresh_semaphore.at[out_row, k])
            )
            fresh[out_row, k] = value
            pltpu.make_async_copy(
                fresh.at[out_row, k], outs[k].at[0, slot], fresh_semaphore.at[out_row, k]
            ).start()
        return carried

    lax.fori_loop(0, count, step, 0)
    for row in range(behind):
        for k in range(3):
            pl.when(row < count)(
                lambda row=row, k=k: settle(fresh.at[row, k], fresh_semaphore.at[row, k])
            )


def after_kernel(*refs):
    del refs


def pack_kernel(slot_ref, core_ref, weight_ref, *refs):
    outs = refs[-2:]
    half = outs[0].shape[0]
    for t in range(half):
        for which in range(2):
            slot = slot_ref[lax.rem(core_ref[0] + which, 2) * half + t]
            tile = weight_ref[0, jnp.maximum(slot, 0)]
            outs[which][t] = jnp.where(slot >= 0, tile, 0.0).astype(low_type)


def round_kernel(weight_ref, *refs):
    refs[-1][...] = weight_ref[0].astype(low_type)


def gather_rows(rows):
    return lax.all_gather(rows, "tensor", axis=0, tiled=True)


def scatter_rows(rows):
    return lax.psum_scatter(rows, "tensor", scatter_dimension=0, tiled=True)


def collect_rows(rows):
    size = lax.axis_size("tensor")
    return [
        lax.ppermute(rows, "tensor", [((i + s) % size, i) for i in range(size)])
        for s in range(1, size)
    ]


def butterfly(values, axis):
    size = lax.axis_size(axis)
    bit = 1
    while bit < size:
        values = values + lax.ppermute(values, axis, [(i, i ^ bit) for i in range(size)])
        bit *= 2
    return values


CORE, ALONG_X, ALONG_Y = 1, 2, 4


def swap(values):
    size = lax.axis_size("dp")
    return lax.ppermute(values, "dp", [(i, i ^ CORE) for i in range(size)])


def hop(values, second=False):
    size = lax.axis_size("dp")
    along = (ALONG_Y, ALONG_X) if second else (ALONG_X, ALONG_Y)
    return lax.ppermute(values, "dp", [(i, i ^ along[i & CORE]) for i in range(size)])


any_spec = pl.BlockSpec(memory_space=pl.ANY)


def after(values, before):
    if not before:
        return values
    return pl.pallas_call(
        after_kernel,
        in_specs=[any_spec] * (1 + len(before)),
        out_specs=any_spec,
        out_shape=shaped(values.shape, values.dtype),
        input_output_aliases={0: 0},
    )(values, *before)


def region(flag, body, *operands):
    shapes = jax.eval_shape(body, *operands)

    def skipped(*_):
        return jax.tree.map(lambda a: jnp.zeros(a.shape, a.dtype), shapes)

    return lax.cond(flag, body, skipped, *operands)


def add_low(*parts):
    total = parts[0].astype(full_type)
    for part in parts[1:]:
        total = total + part.astype(full_type)
    return total.astype(low_type)


def total_tiles(grads):
    count = lax.axis_size("dp")
    pad = -grads.shape[0] % count
    if pad:
        grads = jnp.pad(grads, ((0, pad), (0, 0), (0, 0)))
    owned = lax.psum_scatter(grads, "dp", scatter_dimension=0, tiled=True)
    return lax.all_gather(owned, "dp", axis=0, tiled=True)


def on_device(
    block_in,
    out_grad,
    bank_w,
    bank_m,
    bank_v,
    norm_w,
    norm_m,
    norm_v,
    router_w,
    router_m,
    router_v,
    expert_ids,
    fill_rank,
    owner_list,
):
    dp_count = lax.axis_size("dp")
    images = lax.axis_size("tensor")
    row_count, model = block_in.shape
    group_rows = expert_ids.shape[0]
    slot_width = bank_w.shape[1]
    head = bank_w.shape[2]
    heads = HEADS // images
    runs = FF // (images * head)
    tile_total = owner_list.shape[0]
    near_tiles = 4 * heads
    far_tiles = tile_total - near_tiles
    pair_count = 2 * group_rows
    tokens = images * ROWS
    assert row_count == SEQ and group_rows == images * SEQ

    me = lax.axis_index("dp")
    paired = dp_count == 8
    core = jnp.bitwise_and(me, CORE if paired else 0).astype(jnp.int32)
    flag = owner_list[0] >= 0
    number = jnp.arange(tile_total, dtype=jnp.int32)
    same = owner_list[:, None] == owner_list[None, :]
    slot = jnp.sum(
        jnp.where(jnp.logical_and(same, number[None, :] < number[:, None]), 1, 0), axis=1
    ).astype(jnp.int32)
    near_slots = min(near_tiles, slot_width)
    far_slots = slot_width - near_slots
    owners = jnp.arange(dp_count, dtype=jnp.int32)
    if paired:
        owners = jnp.bitwise_xor(owners, me)
    tile_at = jnp.logical_and(
        owner_list[None, None, :] == owners[:, None, None],
        slot[None, None, :] == jnp.arange(slot_width, dtype=jnp.int32)[None, :, None],
    )
    tile_at = jnp.sum(jnp.where(tile_at, number[None, None, :] + 1, 0), axis=2) - 1
    tile_at = tile_at.astype(jnp.int32)
    slot_here = jnp.where(owner_list == me, slot, -1)
    slot_here = slot_here.astype(jnp.int32)
    slot_number = jnp.arange(slot_width, dtype=jnp.int32)
    slot_used = jnp.sum(
        jnp.where(slot_here[None, :] == slot_number[:, None], 1, 0), axis=1
    ).astype(jnp.int32)

    full_rows = pl.BlockSpec((ROWS, model), lambda *_: (0, 0))
    small = whole((4, model))
    low_rows = shaped((ROWS, model), low_type)
    wide_rows = shaped((ROWS, model), full_type)

    scaled_rows = call(
        first_kernel,
        (1,),
        [full_rows, full_rows],
        whole((ROWS, 2 * model)),
        shaped((ROWS, 2 * model), low_type),
    )(block_in, out_grad)
    both = gather_rows(scaled_rows)
    scaled_half = pl.BlockSpec((ROWS, model), lambda s, *_: (s, 0))
    grads_half = pl.BlockSpec((tokens, model), lambda *_: (0, 1))
    image_rows = pl.BlockSpec((ROWS, model), lambda s, *_: (s, 0))

    group = slot_width // 2 if slot_width % 2 == 0 else 1
    slab = call(
        round_kernel,
        (slot_width // group,),
        [pl.BlockSpec((1, group, head, model), lambda j: (0, j, 0, 0)), any_spec],
        pl.BlockSpec((group, head, model), lambda j: (j, 0, 0)),
        shaped((slot_width, head, model), low_type),
    )(bank_w, scaled_rows)

    keys = (expert_ids * pair_count + fill_rank).astype(full_type).reshape(images, SEQ, 2)
    keys = jnp.pad(
        keys, ((0, 0), (0, ROWS - SEQ), (0, 0)), constant_values=float(2 * EXPERTS * pair_count)
    ).reshape(tokens, 2)
    router_rows = jnp.pad(router_w.astype(low_type).T, ((0, ROUTER_ROWS - EXPERTS), (0, 0)))

    half = near_tiles // 2
    half_shape = (half, head, model)

    def dispatch(keys):
        return call(
            functools.partial(dispatch_kernel, pair_count),
            (EXPERTS,),
            [whole((tokens, 2)), whole((2, tokens))],
            [
                pl.BlockSpec((1, SLOTS, tokens), lambda e: (e, 0, 0)),
                whole((tokens, EXPERTS * SLOTS)),
            ],
            [
                shaped((EXPERTS, SLOTS, tokens), low_type),
                shaped((tokens, EXPERTS * SLOTS), low_type),
            ],
            scratch=[pltpu.VMEM((2, tokens), full_type), pltpu.VMEM((tokens, 2), full_type)],
        )(keys, keys.T)

    if paired:
        near, beside = call(
            pack_kernel,
            (1,),
            [pl.BlockSpec((1, near_slots, head, model), lambda j, *_: (0, 0, 0, 0)), any_spec],
            [whole(half_shape)] * 2,
            [shaped(half_shape, low_type)] * 2,
            prefetch=2,
        )(slot_here[:near_tiles], core.reshape(1), bank_w, slab)
        pick, place = dispatch(keys)
        near = add_low(near, swap(beside))
        near = add_low(near, hop(near))
        slab_beside = after(swap(slab), [near])
        first = hop(slab)
        first_beside = hop(slab_beside)
        near = after(add_low(near, hop(near, second=True)), [both, pick])
        near_banks = [near, swap(near)]
        near_table = jnp.concatenate(
            [jnp.arange(half, dtype=jnp.int32) + lax.rem(core + i, 2) * half for i in range(2)]
        )
    else:
        pick, place = dispatch(keys)
        near_banks = [lax.all_gather(slab, "dp", axis=0, tiled=True)]
        near_table = tile_at.reshape(-1)

    width = heads * head
    all_rows = whole((tokens, model))
    all_shape = shaped((tokens, model), low_type)
    mixed_shape = (images, ROWS, 3 * width)
    attended_shape = (images, ROWS, width)
    mixed_spec = pl.BlockSpec((1,) + mixed_shape[1:], lambda s, *_: (s, 0, 0))
    attended_spec = pl.BlockSpec((1,) + attended_shape[1:], lambda s, *_: (s, 0, 0))
    normed, mixed, attended, branch = call(
        functools.partial(attend_kernel, heads, len(near_banks)),
        (images,),
        [any_spec] * len(near_banks) + [scaled_half, small, any_spec],
        [image_rows, mixed_spec, attended_spec, image_rows],
        [all_shape, shaped(mixed_shape, low_type), shaped(attended_shape, low_type), all_shape],
        scratch=[pltpu.VMEM((near_tiles, head, model), low_type), pltpu.SemaphoreType.DMA(())],
        prefetch=1,
    )(near_table, *near_banks, both, norm_w, slab)
    residual, second_rows = call(
        second_kernel,
        (1,),
        [full_rows, small, full_rows],
        [full_rows, full_rows],
        [wide_rows, low_rows],
    )(block_in, norm_w, scatter_rows(branch))
    picked_grads = call(
        pick_kernel,
        (EXPERTS,),
        [grads_half, pl.BlockSpec((1, SLOTS, tokens), lambda e: (e, 0, 0)), any_spec],
        pl.BlockSpec((1, SLOTS, model), lambda e: (e, 0, 0)),
        shaped((EXPERTS, SLOTS, model), low_type),
    )(both, pick, second_rows)
    second = gather_rows(second_rows)
    mine = jnp.where(core == 0, ALONG_X, ALONG_Y)
    other = ALONG_X + ALONG_Y - mine
    far_away = ALONG_X + ALONG_Y
    if paired:
        first = after(first, [first_beside])
        across = after(hop(first, second=True), [picked_grads])
        far_pieces = [
            (0, 0, slab),
            (CORE, 0, slab_beside),
            (mine, 0, first),
            (mine + CORE, 0, first_beside),
            (far_away, 0, across),
            (other + CORE, 0, swap(first)),
            (other, 0, swap(first_beside)),
        ]
        cuts = 4 if slot_width % 4 == 0 else 1
        size = slot_width // cuts
        far_pieces += [
            (far_away + CORE, i, swap(across[i : i + size])) for i in range(0, slot_width, size)
        ]
        far_banks = [p for _, _, p in far_pieces]
        far_table = jnp.concatenate(
            [
                lax.dynamic_index_in_dim(tile_at, r, 0, keepdims=False)[f : f + p.shape[0]]
                for r, f, p in far_pieces
            ]
        )
    else:
        far_banks, far_table = near_banks, near_table

    near_here = slot_here[:near_tiles]

    def plan(wanted, table):
        place = jnp.cumsum(wanted) - 1
        listed = jnp.logical_and(wanted[None, :] == 1, place[None, :] == slot_number[:, None])
        slots = jnp.sum(jnp.where(listed, slot_number[None, :], 0), axis=1).astype(jnp.int32)
        count = jnp.sum(wanted).astype(jnp.int32).reshape(1)
        return jnp.concatenate([slots, slot_used, count, table])

    if paired:

        def far_tables(*order):
            return jnp.concatenate(
                [
                    lax.dynamic_slice_in_dim(
                        slot_here, near_tiles + jnp.bitwise_xor(me, r) * runs, runs, 0
                    )
                    for r in order
                ]
            )

        def held(table):
            return jnp.sum(
                jnp.where(table[None, :] == slot_number[:, None], 1, 0), axis=1
            ).astype(jnp.int32)

        tables = [
            far_tables(0, CORE, mine, other + CORE),
            far_tables(mine + CORE, other, far_away, far_away + CORE),
            jnp.concatenate(
                [
                    lax.dynamic_slice_in_dim(near_here, lax.rem(core + i, 2) * half, half, 0)
                    for i in range(2)
                ]
            ),
        ]
        wanted = [held(table) for table in tables]
        tables.append(jnp.zeros((0,), jnp.int32))
        wanted.append(1 - slot_used)
        plans = [after(plan(w, t), [second_rows]) for w, t in zip(wanted, tables)]
    else:
        plans = []

    def update(table, sources, olds):
        ahead, behind = 4, 3
        return pl.pallas_call(
            functools.partial(bank_kernel, len(sources)),
            grid_spec=pltpu.PrefetchScalarGridSpec(
                num_scalar_prefetch=1,
                grid=(1,),
                in_specs=[any_spec] * (3 + len(sources) + len(olds)),
                out_specs=[any_spec] * 3,
                scratch_shapes=[
                    pltpu.VMEM((ahead, 3, head, model), full_type),
                    pltpu.VMEM((behind, 3, head, model), full_type),
                    pltpu.VMEM((slot_width, head, model), low_type),
                    pltpu.SemaphoreType.DMA((ahead, 3)),
                    pltpu.SemaphoreType.DMA((behind, 3)),
                    pltpu.SemaphoreType.DMA((slot_width,)),
                ],
            ),
            out_shape=[shaped(bank_w.shape, full_type)] * 3,
            input_output_aliases={4 + len(sources) + i: i for i in range(len(olds))},
            compiler_params=pltpu.CompilerParams(vmem_limit_bytes=VMEM_BYTES),
        )(table, bank_w, bank_m, bank_v, *sources, *olds)

    blocks = 2 * EXPERTS
    tiles_shape = (runs, head, model)
    half_blocks = (EXPERTS,) + tiles_shape
    block_number = jnp.arange(blocks, dtype=jnp.int32)
    if paired:
        order = [far_away + CORE, other, other + CORE, CORE, far_away, mine + CORE, mine, 0]
        order = jnp.bitwise_xor(me, jnp.stack([jnp.asarray(r, me.dtype) for r in order]))
        place_of = jnp.sum(
            jnp.where(order[None, :] == block_number[:, None], block_number[None, :], 0), axis=1
        )
    else:
        place_of = block_number
    expert_rows = pl.BlockSpec((1, SLOTS, model), lambda e, *_: (e, 0, 0))
    piece_shape = (ROWS + ROUTER_ROWS, model)
    pieces_shape = (images * piece_shape[0], model)
    expert_tiles = (EXPERTS, 2 * runs, head, model)

    tiles = call(
        functools.partial(prepare_kernel, near_tiles, len(far_banks)),
        (1,),
        [any_spec] * (len(far_banks) + 1 + len(plans)),
        whole((far_tiles, head, model)),
        shaped((far_tiles, head, model), low_type),
        scratch=[pltpu.SemaphoreType.DMA(())],
        prefetch=1,
    )(far_table, *far_banks, second_rows, *plans)
    sent_first, sent, kept, gated, pieces = call(
        functools.partial(expert_kernel, images, runs),
        (EXPERTS,),
        [
            pl.BlockSpec((1,) + expert_tiles[1:], lambda e, *_: (e, 0, 0, 0)),
            expert_rows,
            all_rows,
            whole((ROUTER_ROWS, model)),
            pl.BlockSpec((1, SLOTS, tokens), lambda e, *_: (e, 0, 0)),
            any_spec,
        ],
        [any_spec, any_spec, any_spec, expert_rows, whole(pieces_shape)],
        [
            shaped(tiles_shape, low_type),
            shaped((EXPERTS - 1,) + tiles_shape, low_type),
            shaped(half_blocks, low_type),
        ]
        + [shaped((EXPERTS, SLOTS, model), low_type), shaped(pieces_shape, low_type)],
        scratch=[
            pltpu.VMEM((ROUTER_ROWS, tokens), full_type),
            pltpu.VMEM((ROUTER_ROWS, tokens), full_type),
            pltpu.VMEM((EXPERTS * SLOTS, model), low_type),
            pltpu.VMEM((tokens, EXPERTS * SLOTS), low_type),
            pltpu.VMEM((2, 2) + tiles_shape, low_type),
            pltpu.SemaphoreType.DMA((2, 2)),
            pltpu.SemaphoreType.DMA(()),
        ],
        prefetch=1,
    )(
        place_of.astype(jnp.int32),
        tiles.reshape(expert_tiles),
        picked_grads,
        second,
        router_rows,
        pick,
        place,
    )
    piece = scatter_rows(pieces)

    def combine(gated):
        return call(
            combine_kernel,
            (images,),
            [
                whole((EXPERTS * SLOTS, model)),
                pl.BlockSpec((ROWS, EXPERTS * SLOTS), lambda s: (s, 0)),
            ],
            image_rows,
            all_shape,
        )(gated.reshape(EXPERTS * SLOTS, model), place)

    def sum_far(sent_first, sent, kept, gated):
        across = add_low(kept[0], swap(sent_first))
        part = swap(after(sent, [across]))
        across = hop(across, second=True)
        combined = combine(gated)
        beside = hop(add_low(kept[1], part[0]))
        return combined, part, beside, add_low(kept[2], part[1], across)

    if paired:
        combined, part, beside, along = region(flag, sum_far, sent_first, sent, kept, gated)
        ordered = [along]
    else:
        combined, ordered = combine(gated), []

    residual_grad, branch_rows, small_two = call(
        second_back_kernel,
        (1,),
        [full_rows, full_rows, full_rows, whole((ROUTER_ROWS, model)), small, whole(piece_shape)]
        + [any_spec] * len(ordered),
        [full_rows, full_rows, whole((8, model))],
        [wide_rows, low_rows, shaped((8, model), full_type)],
    )(residual, out_grad, second_rows, router_rows, norm_w, piece, *ordered)
    branch_grads = gather_rows(branch_rows)

    if paired:

        def sum_own(kept, part, beside, along, plan):
            own = add_low(kept[3], part[2], hop(along), swap(beside))
            return update(plan, [], []), own, swap(own), hop(own)

        own_blocks = region(
            flag, sum_own, kept, part, beside, after(along, [branch_rows]), plans[3]
        )
    else:
        products = jnp.concatenate([sent_first[None], sent, kept], axis=0)
        products = products.reshape(far_tiles, head, model)
        far_sources = [total_tiles(products)]
        far_slots_here = [
            jnp.pad(
                slot_here[near_tiles:],
                (0, far_sources[0].shape[0] - far_tiles),
                constant_values=-1,
            )
        ]

    here = lax.axis_index("tensor").astype(jnp.int32).reshape(1)
    near_rows = half * head
    near_shape = (near_rows + 16, model)
    def add_near(left, right, before=(), apart=False):
        shapes = [(near_rows, model), (16, model)] if apart else [near_shape]
        out = call(
            functools.partial(near_add_kernel, len(shapes)),
            (1,),
            [whole(near_shape)] * 2 + [any_spec] * len(before),
            [whole(shape) for shape in shapes],
            [shaped(shape, low_type) for shape in shapes],
        )(left, right, *before)
        return out if apart else out[0]

    def attend_back(branch_grads, small_two):
        return call(
            functools.partial(attend_back_kernel, images, heads, len(near_banks)),
            (images,),
            [any_spec] * len(near_banks)
            + [image_rows, scaled_half, image_rows, mixed_spec, attended_spec]
            + [whole((8, model))],
            [whole(near_shape)] * 2 + [image_rows, whole((8, model))],
            [shaped(near_shape, low_type)] * 2 + [all_shape, shaped((8, model), full_type)],
            scratch=[
                pltpu.VMEM((near_tiles, head, model), low_type),
                pltpu.VMEM((tokens, model), low_type),
                pltpu.VMEM((tokens, model), low_type),
                pltpu.VMEM((tokens, 3 * width), low_type),
                pltpu.VMEM((tokens, width), low_type),
                pltpu.SemaphoreType.DMA(()),
            ],
            prefetch=2,
        )(
            near_table,
            core.reshape(1),
            *near_banks,
            branch_grads,
            both,
            normed,
            mixed,
            attended,
            small_two,
        )

    def third(branch_grads, small_two, plan, banks, own, own_beside, first):
        far = [hop(own_beside), hop(first, second=True)]
        early = [own, own_beside, first, swap(first)]
        near, beside, pieces, _ = attend_back(branch_grads, small_two)
        near = add_near(near, swap(beside))
        return near, pieces, far, update(plan, early, banks)

    combined = scatter_rows(combined)
    if paired:
        near, pieces, far, banks = region(
            flag, third, branch_grads, small_two, plans[0], *own_blocks
        )
        pieces = after(pieces, [combined])
    else:
        near_own, near_beside, pieces, sums = attend_back(branch_grads, small_two)
    pieces = scatter_rows(pieces)

    def finish(far, own, banks, plans):
        late = [p for block in far for p in (block, swap(block))]
        banks = update(plans[0], late, banks)
        own, sums = add_near(own, hop(own), banks[:1], apart=True)
        sums = [sums] + collect_rows(sums)
        sums = call(
            functools.partial(last_sum_kernel, images),
            (1,),
            [whole((16, model))] * images,
            whole((8, model)),
            shaped((8, model), full_type),
            scratch=[pltpu.VMEM((images, 8, model), full_type)],
            prefetch=1,
        )(here, *sums)
        own = add_low(own, after(hop(own, second=True), [sums]))
        tiles_here = own.reshape(half_shape)
        other_sums = hop(sums, second=True)
        banks = update(plans[1], [tiles_here, swap(tiles_here)], banks)
        sums = sums + after(other_sums, [banks[2]])
        return *banks, sums

    if paired:
        bank_first, bank_second, bank_new, sums = region(
            flag, finish, far, near, banks, plans[1:3]
        )
    else:
        near_grads = jnp.concatenate([near_own[:near_rows], near_beside[:near_rows]], axis=0)
        near_sources = [total_tiles(near_grads.reshape(near_tiles, head, model))]
        near_slots_here = [
            jnp.pad(near_here, (0, near_sources[0].shape[0] - near_tiles), constant_values=-1)
        ]
        sums = butterfly(butterfly(sums, "tensor"), "dp")
        table = jnp.concatenate([far_slots_here[0], near_slots_here[0]])
        bank_first, bank_second, bank_new = update(
            plan(jnp.ones((slot_width,), jnp.int32), table), far_sources + near_sources, []
        )
    input_grad, block_out = call(
        first_back_kernel,
        (1,),
        [full_rows, full_rows, small, full_rows, full_rows, full_rows, any_spec],
        [full_rows, full_rows],
        [shaped((SEQ, model), full_type)] * 2,
    )(block_in, residual_grad, norm_w, residual, pieces, combined, bank_new)
    norm_grad = sums[:4]
    router_total = sums[4:].T
    norm_first, norm_second, norm_new = adamw_update(
        norm_w, norm_m, norm_v, norm_grad, rate_norm, 0.0
    )
    router_first, router_second, router_new = adamw_update(
        router_w, router_m, router_v, router_total, rate_router, weight_decay
    )
    return (
        block_out,
        input_grad,
        bank_first,
        bank_second,
        bank_new,
        norm_first,
        norm_second,
        norm_new,
        router_first,
        router_second,
        router_new,
    )


def solution(mesh):
    rows = P(("dp", "tensor"), None)
    bank = P("tensor", "dp", None, None)
    return jax.shard_map(
        on_device,
        mesh=mesh,
        in_specs=(rows, rows, bank, bank, bank) + (P(),) * 6 + (P("dp", None), P("dp", None), P()),
        out_specs=(rows, rows, bank, bank, bank) + (P(),) * 6,
        check_vma=False,
    )
```

```python
import functools

import jax
import jax.numpy as jnp
from jax import lax
from jax.experimental import pallas as pl
from jax.experimental.pallas import tpu as pltpu
from jax.sharding import PartitionSpec as P

HEADS = 12
FF = 3072
SEQ = 197
EXPERTS = 4
STEP = 10
CAPACITY = 443

ROWS = -(-SEQ // 16) * 16
SLOTS = -(-CAPACITY // 16) * 16
ROUTER_ROWS = 16
VMEM_BYTES = 56 * 1024 * 1024

norm_epsilon = 1e-06
beta_first = 0.9
beta_second = 0.95
adam_epsilon = 1e-08
weight_decay = 0.1
rate_bank = 0.06
rate_norm = 0.25
rate_router = 0.05
highest = lax.Precision.HIGHEST
low_type = jnp.bfloat16
full_type = jnp.float32


def dot_nn(left, right):
    return lax.dot_general(left, right, (((1,), (0,)), ((), ())), preferred_element_type=full_type)


def dot_nt(left, right):
    return lax.dot_general(left, right, (((1,), (1,)), ((), ())), preferred_element_type=full_type)


def dot_tn(left, right):
    return lax.dot_general(left, right, (((0,), (0,)), ((), ())), preferred_element_type=full_type)


def adamw_update(weights, first_old, second_old, grad_total, step_rate, decay_rate):
    first_new = beta_first * first_old + (1.0 - beta_first) * grad_total
    second_new = beta_second * second_old + (1.0 - beta_second) * grad_total * grad_total
    first_scale = step_rate / (1.0 - beta_first**STEP)
    second_scale = 1.0 / (1.0 - beta_second**STEP)
    weights_new = weights * (1.0 - step_rate * decay_rate) - first_new * first_scale / (
        jnp.sqrt(second_new * second_scale) + adam_epsilon
    )
    return (first_new, second_new, weights_new)


def call(body, grid, in_specs, out_specs, out_shape, scratch=(), prefetch=0, flops=0, moved=0):
    return pl.pallas_call(
        body,
        grid_spec=pltpu.PrefetchScalarGridSpec(
            num_scalar_prefetch=prefetch,
            grid=grid,
            in_specs=in_specs,
            out_specs=out_specs,
            scratch_shapes=list(scratch),
        ),
        out_shape=out_shape,
        compiler_params=pltpu.CompilerParams(vmem_limit_bytes=VMEM_BYTES),
        cost_estimate=pl.CostEstimate(flops=flops, bytes_accessed=moved, transcendentals=0),
    )


def whole(shape):
    return pl.BlockSpec(shape, lambda *_: (0,) * len(shape))


def shaped(shape, kind):
    return jax.ShapeDtypeStruct(shape, kind)


def row_mask(rows):
    return lax.broadcasted_iota(jnp.int32, (rows, 1), 0) < SEQ


def normalize(values):
    center = values - jnp.mean(values, axis=-1, keepdims=True)
    variance = jnp.mean(center * center, axis=-1, keepdims=True)
    spread = lax.rsqrt(variance + norm_epsilon)
    return center * spread, spread


def norm_back(scaled, spread, grad_rows, gain_row):
    inner = grad_rows * gain_row
    mean_one = jnp.mean(inner, axis=-1, keepdims=True)
    mean_two = jnp.mean(inner * scaled, axis=-1, keepdims=True)
    return spread * (inner - mean_one - scaled * mean_two)


def first_kernel(block_ref, grad_ref, out_ref):
    mask = row_mask(ROWS)
    model = block_ref.shape[1]
    scaled, _ = normalize(jnp.where(mask, block_ref[...], 0.0))
    out_ref[:, :model] = jnp.where(mask, scaled, 0.0).astype(low_type)
    out_ref[:, model:] = jnp.where(mask, grad_ref[...], 0.0).astype(low_type)


def dispatch_kernel(pair_count, col_ref, row_ref, pick_ref, place_ref, slot_row, slot_col):
    expert = pl.program_id(0)
    tokens = row_ref.shape[1]
    chunk = ROWS // 2

    @pl.when(expert == 0)
    def _():
        row_zero = row_ref[0:1, :]
        row_one = row_ref[1:2, :]

        def ones(condition):
            return jnp.where(condition, 1.0, 0.0)

        bounds = [float(e * pair_count) for e in range(1, EXPERTS)]
        below = [
            jnp.sum(ones(row_zero < b) + ones(row_one < b), axis=1, keepdims=True) for b in bounds
        ]

        def slots(keys, lower):
            base = jnp.zeros_like(keys)
            index = jnp.zeros_like(keys)
            for bound, count in zip(bounds, below):
                base = jnp.where(keys >= bound, jnp.broadcast_to(count, keys.shape), base)
                index = index + ones(keys >= bound)
            placed = lower - base
            kept = jnp.logical_and(placed < CAPACITY, keys < float(EXPERTS * pair_count))
            return jnp.where(kept, index * SLOTS + placed, -1.0)

        def step(i, carried):
            low_zero, low_one = carried
            start = pl.multiple_of(i * chunk, 8)
            keys = col_ref[pl.ds(start, chunk), :]
            zero = keys[:, 0:1]
            one = keys[:, 1:2]
            before_zero = jnp.sum(
                ones(row_zero < zero) + ones(row_one < zero), axis=1, keepdims=True
            )
            before_one = jnp.sum(ones(row_zero < one) + ones(row_one < one), axis=1, keepdims=True)
            slot_col[pl.ds(start, chunk), 0:1] = slots(zero, before_zero)
            slot_col[pl.ds(start, chunk), 1:2] = slots(one, before_one)
            low_zero = low_zero + jnp.sum(
                ones(zero < row_zero) + ones(one < row_zero), axis=0, keepdims=True
            )
            low_one = low_one + jnp.sum(
                ones(zero < row_one) + ones(one < row_one), axis=0, keepdims=True
            )
            return low_zero, low_one

        nothing = jnp.zeros((1, tokens), full_type)
        low_zero, low_one = lax.fori_loop(0, tokens // chunk, step, (nothing, nothing))
        slot_row[0:1, :] = slots(row_zero, low_zero)
        slot_row[1:2, :] = slots(row_one, low_one)

    begin = expert * SLOTS
    down = (lax.broadcasted_iota(jnp.int32, (SLOTS, 1), 0) + begin).astype(full_type)
    hit = jnp.logical_or(slot_row[0:1, :] == down, slot_row[1:2, :] == down)
    pick_ref[0] = jnp.where(hit, 1.0, 0.0).astype(low_type)

    @pl.when(expert == 0)
    def _():
        across = lax.broadcasted_iota(jnp.int32, (1, EXPERTS * SLOTS), 1).astype(full_type)
        hit = jnp.logical_or(slot_col[:, 0:1] == across, slot_col[:, 1:2] == across)
        place_ref[...] = jnp.where(hit, 1.0, 0.0).astype(low_type)


def fetch_tiles(table_ref, pieces, first, last, start, offset=0):
    for piece in pieces:

        def step(j, carried, piece=piece, offset=offset):
            tile = table_ref[offset + j]

            @pl.when(jnp.logical_and(tile >= first, tile < last))
            def _():
                start(piece.at[j], tile)

            return carried

        lax.fori_loop(0, piece.shape[0], step, 0)
        offset += piece.shape[0]


def softmax_rows(scores):
    valid = lax.broadcasted_iota(jnp.int32, scores.shape, 1) < SEQ
    scores = jnp.where(valid, scores, -1e30)
    top = jnp.max(scores, axis=-1, keepdims=True)
    powers = jnp.exp(scores - top)
    return powers / jnp.sum(powers, axis=-1, keepdims=True)


def attend_kernel(heads, banks, table_ref, *refs):
    bank, refs = refs[:banks], refs[banks:]
    scaled_ref, norm_ref = refs[:2]
    normed_ref, mixed_ref, attended_ref, branch_ref, tiles, semaphore = refs[-6:]
    count, head, model = tiles.shape

    @pl.when(pl.program_id(0) == 0)
    def _():
        def start(source, tile):
            pltpu.make_async_copy(source, tiles.at[tile], semaphore).start()

        fetch_tiles(table_ref, bank, 0, count, start)
        pltpu.make_async_copy(tiles, tiles, semaphore).wait()

    width = heads * head
    proj_in = tiles[: 3 * heads].reshape(3 * width, model)
    proj_out = tiles[3 * heads :].reshape(width, model)
    mask = row_mask(ROWS)
    rows = scaled_ref[...].astype(full_type) * norm_ref[0:1, :] + norm_ref[1:2, :]
    rows = jnp.where(mask, rows, 0.0).astype(low_type)
    normed_ref[...] = rows
    mixed = dot_nt(rows, proj_in).astype(low_type)
    mixed_ref[0] = mixed
    parts = []
    for h in range(heads):
        query, key, value = (
            mixed[:, p * width + h * head : p * width + (h + 1) * head] for p in range(3)
        )
        probs = softmax_rows(dot_nt(query, key) * head**-0.5).astype(low_type)
        parts.append(dot_nn(probs, value))
    attended = jnp.where(mask, jnp.concatenate(parts, axis=1), 0.0).astype(low_type)
    attended_ref[0] = attended
    branch_ref[...] = dot_nn(attended, proj_out).astype(low_type)


def second_kernel(block_ref, norm_ref, branch_ref, residual_ref, second_ref):
    mask = row_mask(ROWS)
    residual = jnp.where(mask, block_ref[...], 0.0) + branch_ref[...].astype(full_type)
    residual_ref[...] = residual
    scaled, _ = normalize(residual)
    rows = scaled * norm_ref[2:3, :] + norm_ref[3:4, :]
    second_ref[...] = jnp.where(mask, rows, 0.0).astype(low_type)


def gelu_pair(values):
    factor = 0.7978845608028654
    square = values * values
    bent = jnp.tanh(factor * values * (1.0 + 0.044715 * square))
    half = 0.5 * (1.0 + bent)
    slope = half + 0.5 * factor * values * (1.0 - bent * bent) * (1.0 + 0.134145 * square)
    return values * half, slope


def expert_probs(router_rows, second_rows):
    logits = dot_nt(router_rows, second_rows)
    real = lax.broadcasted_iota(jnp.int32, logits.shape, 0) < EXPERTS
    logits = jnp.where(real, logits, -1e30)
    powers = jnp.exp(logits - jnp.max(logits, axis=0, keepdims=True))
    return powers / jnp.sum(powers, axis=0, keepdims=True)


def pick_kernel(cotangent_ref, pick_ref, _, rows_ref):
    rows_ref[0] = dot_nn(pick_ref[0], cotangent_ref[...]).astype(low_type)


def prepare_kernel(base, banks, table_ref, *refs):
    bank = refs[:banks]
    tiles_ref, semaphore = refs[-2:]
    count = tiles_ref.shape[0]

    def copy(source, tile):
        return pltpu.make_async_copy(source, tiles_ref.at[tile - base], semaphore.at[tile - base])

    fetch_tiles(table_ref, bank, base, base + count, lambda *a: copy(*a).start())
    fetch_tiles(table_ref, bank, base, base + count, lambda *a: copy(*a).wait())


def place_kernel(base, banks, table_ref, *refs):
    bank = refs[:banks]
    tiles_ref, held, read_semaphore, write_semaphore = refs[-4:]
    count = tiles_ref.shape[0]

    def read(source, tile):
        return pltpu.make_async_copy(source, held.at[tile - base], read_semaphore.at[tile - base])

    def write(_, tile):
        place = tile - base
        return pltpu.make_async_copy(held.at[place], tiles_ref.at[place], write_semaphore.at[place])

    def settle(source, tile):
        read(source, tile).wait()
        write(source, tile).start()

    fetch_tiles(table_ref, bank, base, base + count, lambda *a: read(*a).start())
    fetch_tiles(table_ref, bank, base, base + count, settle)
    fetch_tiles(table_ref, bank, base, base + count, lambda *a: write(*a).wait())


def expert_kernel(images, runs, place_of_ref, *refs):
    tiles_ref, grads_ref, second_ref, router_ref, pick_ref, place_ref = refs[:6]
    first_ref, sent_ref, kept_ref, gated_ref, piece_ref = refs[6:11]
    probs, pair_grad, rows_back, place, stage, out_semaphore, place_semaphore = refs[11:]
    expert = pl.program_id(0)
    model = second_ref.shape[1]
    hidden_width = runs * tiles_ref.shape[2]
    place_copy = pltpu.make_async_copy(place_ref, place, place_semaphore)

    @pl.when(expert == 0)
    def _():
        place_copy.start()
        probs[...] = expert_probs(router_ref[...], second_ref[...])
        pair_grad[...] = jnp.zeros_like(pair_grad)

    weight_in = tiles_ref[0, :runs].reshape(hidden_width, model)
    weight_out = tiles_ref[0, runs:].reshape(hidden_width, model)
    pick = pick_ref[0]
    pick_full = pick.astype(full_type)
    gate = jnp.sum(pick_full * probs[pl.ds(expert, 1), :], axis=1, keepdims=True)
    grad_rows = grads_ref[0].astype(full_type)
    back = (gate * grad_rows).astype(low_type)
    rows = dot_nn(pick, second_ref[...]).astype(low_type)
    hidden = dot_nt(rows, weight_in)
    act_grad = dot_nt(back, weight_out)
    activated, slope = gelu_pair(hidden)
    activated = activated.astype(low_type)
    hidden_grad = (act_grad * slope).astype(low_type)
    returned = dot_nn(activated, weight_out)
    here = pl.ds(pl.multiple_of(expert * SLOTS, SLOTS), SLOTS)
    rows_back[here, :] = dot_nn(hidden_grad, weight_in).astype(low_type)
    gate_grad = jnp.sum(grad_rows * returned, axis=1, keepdims=True)
    pair_grad[pl.ds(expert, 1), :] = jnp.sum(pick_full * gate_grad, axis=0, keepdims=True)
    gated_ref[0] = (gate * returned).astype(low_type)
    slot = lax.rem(expert, 2)
    sent_count = 1 + sent_ref.shape[0]

    def settle(which, m):
        copy = stage.at[which, m]
        pltpu.make_async_copy(copy, copy, out_semaphore.at[which, m]).wait()

    for m, (left, right) in enumerate(((hidden_grad, rows), (activated, back))):

        @pl.when(expert >= 2)
        def _(m=m):
            settle(slot, m)

        stage[slot, m] = dot_tn(left, right).astype(low_type).reshape(stage.shape[2:])
        target = place_of_ref[2 * expert + m]
        copy = (stage.at[slot, m], out_semaphore.at[slot, m])

        @pl.when(target == 0)
        def _(copy=copy):
            pltpu.make_async_copy(copy[0], first_ref, copy[1]).start()

        @pl.when(jnp.logical_and(target > 0, target < sent_count))
        def _(target=target, copy=copy):
            pltpu.make_async_copy(copy[0], sent_ref.at[target - 1], copy[1]).start()

        @pl.when(target >= sent_count)
        def _(target=target, copy=copy):
            pltpu.make_async_copy(copy[0], kept_ref.at[target - sent_count], copy[1]).start()

    @pl.when(expert == EXPERTS - 1)
    def _():
        place_copy.wait()
        total = dot_nn(place[...], rows_back[...])
        for s in range(images):
            first = s * (ROWS + ROUTER_ROWS)
            last = first + ROWS + ROUTER_ROWS
            middle = first + ROWS
            here = slice(s * ROWS, (s + 1) * ROWS)
            piece_ref[first:middle, :] = total[here, :].astype(low_type)
            piece_ref[middle:last, :] = jnp.zeros((ROUTER_ROWS, model), low_type)
            piece_ref[middle:last, :ROWS] = pair_grad[:, here].astype(low_type)
        for which in range(2):
            for m in range(2):
                settle(which, m)


def combine_kernel(gated_ref, place_ref, out_ref):
    out_ref[...] = dot_nn(place_ref[...], gated_ref[...]).astype(low_type)


def second_back_kernel(
    residual_ref, grad_ref, second_ref, router_ref, norm_ref, piece_ref, *refs
):
    rows_ref, low_ref, small_ref = refs[-3:]
    mask = row_mask(ROWS)
    total = piece_ref[...].astype(full_type)
    second = second_ref[...]
    router_rows = router_ref[...]
    probs = expert_probs(router_rows, second)
    probs_grad = total[ROWS:, :ROWS]
    logit_grad = probs * (probs_grad - jnp.sum(probs * probs_grad, axis=0, keepdims=True))
    second_grad = total[:ROWS, :] + lax.dot_general(
        logit_grad,
        router_rows.astype(full_type),
        (((0,), (0,)), ((), ())),
        precision=highest,
        preferred_element_type=full_type,
    )
    router_grad = lax.dot_general(
        logit_grad,
        second.astype(full_type),
        (((1,), (0,)), ((), ())),
        precision=highest,
        preferred_element_type=full_type,
    )
    second_grad = jnp.where(mask, second_grad, 0.0)
    scaled, spread = normalize(residual_ref[...])
    part = norm_back(scaled, spread, second_grad, norm_ref[2:3, :])
    rows = jnp.where(mask, grad_ref[...] + part, 0.0)
    rows_ref[...] = rows
    low_ref[...] = rows.astype(low_type)
    small_ref[0:1, :] = jnp.sum(second_grad * scaled, axis=0, keepdims=True)
    small_ref[1:2, :] = jnp.sum(second_grad, axis=0, keepdims=True)
    small_ref[2 : 2 + EXPERTS, :] = router_grad[:EXPERTS, :]
    small_ref[2 + EXPERTS :, :] = jnp.zeros((6 - EXPERTS, small_ref.shape[1]), full_type)


def attend_back_kernel(images, heads, banks, table_ref, core_ref, *refs):
    bank, refs = refs[:banks], refs[banks:]
    (
        branch_ref,
        scaled_ref,
        normed_ref,
        mixed_ref,
        attended_ref,
        small_two_ref,
        own_ref,
        other_ref,
        piece_ref,
        small_ref,
        tiles,
        cotangent,
        normed,
        mixed_grad,
        attended,
        semaphore,
    ) = refs
    count, head, model = tiles.shape
    image = pl.program_id(0)

    @pl.when(image == 0)
    def _():
        def start(source, tile):
            pltpu.make_async_copy(source, tiles.at[tile], semaphore).start()

        fetch_tiles(table_ref, bank, 0, count, start)
        pltpu.make_async_copy(tiles, tiles, semaphore).wait()
        small_ref[0:2, :] = jnp.zeros((2, model), full_type)
        small_ref[2:, :] = small_two_ref[:6, :]

    width = heads * head
    scale = head**-0.5
    proj_in = tiles[: 3 * heads].reshape(3 * width, model)
    proj_out = tiles[3 * heads :].reshape(width, model)
    here = pl.ds(pl.multiple_of(image * ROWS, ROWS), ROWS)
    branch = branch_ref[...]
    cotangent[here, :] = branch
    normed[here, :] = normed_ref[...]
    attended[here, :] = attended_ref[0]
    attended_grad = dot_nt(branch, proj_out).astype(low_type)
    mixed = mixed_ref[0]
    parts = [[], [], []]
    for h in range(heads):
        query, key, value = (
            mixed[:, p * width + h * head : p * width + (h + 1) * head] for p in range(3)
        )
        above = attended_grad[:, h * head : (h + 1) * head]
        probs = softmax_rows(dot_nt(query, key) * scale)
        weight_grad = dot_nt(above, value)
        inner = jnp.sum(probs * weight_grad, axis=-1, keepdims=True)
        score_grad = (probs * (weight_grad - inner)).astype(low_type)
        parts[0].append(dot_nn(score_grad, key) * scale)
        parts[1].append(dot_tn(score_grad, query) * scale)
        parts[2].append(dot_tn(probs.astype(low_type), above))
    grads = jnp.concatenate(parts[0] + parts[1] + parts[2], axis=1).astype(low_type)
    mixed_grad[here, :] = grads
    back = dot_nn(grads, proj_in)
    piece_ref[...] = back.astype(low_type)
    small_ref[0:1, :] += jnp.sum(back * scaled_ref[...].astype(full_type), axis=0, keepdims=True)
    small_ref[1:2, :] += jnp.sum(back, axis=0, keepdims=True)

    @pl.when(image == images - 1)
    def _():
        tile_grads = jnp.concatenate(
            [
                dot_tn(mixed_grad[...], normed[...]).astype(low_type),
                dot_tn(attended[...], cotangent[...]).astype(low_type),
            ],
            axis=0,
        )
        rows = count // 2 * head
        rest = tile_grads.reshape(2, rows, model)

        @pl.when(core_ref[0] == 0)
        def _():
            own_ref[:rows, :] = rest[0]
            other_ref[:rows, :] = rest[1]

        @pl.when(core_ref[0] == 1)
        def _():
            own_ref[:rows, :] = rest[1]
            other_ref[:rows, :] = rest[0]

        for ref in (own_ref, other_ref):
            ref[rows:, :] = split_sums(small_ref[...])


def split_sums(rows):
    high = rows.astype(low_type)
    low = (rows - high.astype(full_type)).astype(low_type)
    return jnp.concatenate([high.astype(full_type), low.astype(full_type)], axis=0).astype(low_type)


def join_sums(rows):
    wide = rows.astype(full_type)
    return wide[:8, :] + wide[8:, :]


def near_add_kernel(count, left_ref, right_ref, *refs):
    outs = refs[-count:]
    rows = left_ref.shape[0] - 16
    total = left_ref[:rows, :].astype(full_type) + right_ref[:rows, :].astype(full_type)
    sums = split_sums(join_sums(left_ref[rows:, :]) + join_sums(right_ref[rows:, :]))
    outs[0][:rows, :] = total.astype(low_type)
    outs[-1][outs[-1].shape[0] - 16 :, :] = sums


def last_sum_kernel(images, here_ref, *refs):
    pieces, out_ref, held = refs[:images], refs[-2], refs[-1]
    for s in range(images):
        held[lax.rem(here_ref[0] + s, images)] = join_sums(pieces[s][...])
    total = held[0]
    for s in range(1, images):
        total = total + held[s]
    out_ref[...] = total


def first_back_kernel(block_ref, grad_ref, norm_ref, residual_ref, piece_ref, added_ref, *refs):
    grad_out, block_out = refs[-2:]
    mask = row_mask(ROWS)
    total = jnp.where(mask, piece_ref[...].astype(full_type), 0.0)
    scaled, spread = normalize(jnp.where(mask, block_ref[...], 0.0))
    grad_out[...] = grad_ref[...] + norm_back(scaled, spread, total, norm_ref[0:1, :])
    block_out[...] = residual_ref[...] + added_ref[...].astype(full_type)


def bank_kernel(pieces, plan_ref, *refs):
    olds = refs[:3]
    sources = refs[3 : 3 + pieces]
    outs = refs[-9:-6]
    held, fresh, grads, held_semaphore, fresh_semaphore, grad_semaphore = refs[-6:]
    ahead, behind, width = held.shape[0], fresh.shape[0], grads.shape[0]
    count = plan_ref[2 * width]

    def load(j):
        slot, row = plan_ref[j], lax.rem(j, ahead)
        for k in range(3):
            pltpu.make_async_copy(
                olds[k].at[0, slot], held.at[row, k], held_semaphore.at[row, k]
            ).start()

    def settle(ref, semaphore):
        pltpu.make_async_copy(ref, ref, semaphore).wait()

    for j in range(ahead - 1):
        pl.when(j < count)(functools.partial(load, j))

    def start(source, slot):
        pltpu.make_async_copy(source, grads.at[slot], grad_semaphore.at[slot]).start()

    fetch_tiles(plan_ref, sources, 0, width, start, 2 * width + 1)

    def step(j, carried):
        pl.when(j + ahead - 1 < count)(lambda: load(j + ahead - 1))
        slot, row, out_row = plan_ref[j], lax.rem(j, ahead), lax.rem(j, behind)
        used = plan_ref[width + slot]
        for k in range(3):
            settle(held.at[row, k], held_semaphore.at[row, k])
        pl.when(used == 1)(lambda: settle(grads.at[slot], grad_semaphore.at[slot]))
        grad = jnp.where(used == 1, grads[slot].astype(full_type), 0.0)
        updated = adamw_update(*(held[row, k] for k in range(3)), grad, rate_bank, weight_decay)
        for k, value in enumerate(updated):
            pl.when(j >= behind)(
                lambda k=k: settle(fresh.at[out_row, k], fresh_semaphore.at[out_row, k])
            )
            fresh[out_row, k] = value
            pltpu.make_async_copy(
                fresh.at[out_row, k], outs[k].at[0, slot], fresh_semaphore.at[out_row, k]
            ).start()
        return carried

    lax.fori_loop(0, count, step, 0)
    for row in range(behind):
        for k in range(3):
            pl.when(row < count)(
                lambda row=row, k=k: settle(fresh.at[row, k], fresh_semaphore.at[row, k])
            )


def after_kernel(*refs):
    del refs


def pack_kernel(slot_ref, core_ref, weight_ref, *refs):
    outs = refs[-2:]
    half = outs[0].shape[0]
    for t in range(half):
        for which in range(2):
            slot = slot_ref[lax.rem(core_ref[0] + which, 2) * half + t]
            tile = weight_ref[0, jnp.maximum(slot, 0)]
            outs[which][t] = jnp.where(slot >= 0, tile, 0.0).astype(low_type)


def round_kernel(weight_ref, *refs):
    refs[-1][...] = weight_ref[0].astype(low_type)


def gather_rows(rows):
    return lax.all_gather(rows, "tensor", axis=0, tiled=True)


def scatter_rows(rows):
    return lax.psum_scatter(rows, "tensor", scatter_dimension=0, tiled=True)


def collect_rows(rows):
    size = lax.axis_size("tensor")
    return [
        lax.ppermute(rows, "tensor", [((i + s) % size, i) for i in range(size)])
        for s in range(1, size)
    ]


def butterfly(values, axis):
    size = lax.axis_size(axis)
    bit = 1
    while bit < size:
        values = values + lax.ppermute(values, axis, [(i, i ^ bit) for i in range(size)])
        bit *= 2
    return values


CORE, ALONG_X, ALONG_Y = 1, 2, 4


def swap(values):
    size = lax.axis_size("dp")
    return lax.ppermute(values, "dp", [(i, i ^ CORE) for i in range(size)])


def hop(values, second=False):
    size = lax.axis_size("dp")
    along = (ALONG_Y, ALONG_X) if second else (ALONG_X, ALONG_Y)
    return lax.ppermute(values, "dp", [(i, i ^ along[i & CORE]) for i in range(size)])


any_spec = pl.BlockSpec(memory_space=pl.ANY)


def after(values, before):
    if not before:
        return values
    return pl.pallas_call(
        after_kernel,
        in_specs=[any_spec] * (1 + len(before)),
        out_specs=any_spec,
        out_shape=shaped(values.shape, values.dtype),
        input_output_aliases={0: 0},
    )(values, *before)


def region(flag, body, *operands):
    shapes = jax.eval_shape(body, *operands)

    def skipped(*_):
        return jax.tree.map(lambda a: jnp.zeros(a.shape, a.dtype), shapes)

    return lax.cond(flag, body, skipped, *operands)


def add_low(*parts):
    total = parts[0].astype(full_type)
    for part in parts[1:]:
        total = total + part.astype(full_type)
    return total.astype(low_type)


def total_tiles(grads):
    count = lax.axis_size("dp")
    pad = -grads.shape[0] % count
    if pad:
        grads = jnp.pad(grads, ((0, pad), (0, 0), (0, 0)))
    owned = lax.psum_scatter(grads, "dp", scatter_dimension=0, tiled=True)
    return lax.all_gather(owned, "dp", axis=0, tiled=True)


def on_device(
    block_in,
    out_grad,
    bank_w,
    bank_m,
    bank_v,
    norm_w,
    norm_m,
    norm_v,
    router_w,
    router_m,
    router_v,
    expert_ids,
    fill_rank,
    owner_list,
):
    dp_count = lax.axis_size("dp")
    images = lax.axis_size("tensor")
    row_count, model = block_in.shape
    group_rows = expert_ids.shape[0]
    slot_width = bank_w.shape[1]
    head = bank_w.shape[2]
    heads = HEADS // images
    runs = FF // (images * head)
    tile_total = owner_list.shape[0]
    near_tiles = 4 * heads
    far_tiles = tile_total - near_tiles
    pair_count = 2 * group_rows
    tokens = images * ROWS
    assert row_count == SEQ and group_rows == images * SEQ

    me = lax.axis_index("dp")
    paired = dp_count == 8
    core = jnp.bitwise_and(me, CORE if paired else 0).astype(jnp.int32)
    flag = owner_list[0] >= 0
    number = jnp.arange(tile_total, dtype=jnp.int32)
    same = owner_list[:, None] == owner_list[None, :]
    slot = jnp.sum(
        jnp.where(jnp.logical_and(same, number[None, :] < number[:, None]), 1, 0), axis=1
    ).astype(jnp.int32)
    near_slots = min(near_tiles, slot_width)
    far_slots = slot_width - near_slots
    owners = jnp.arange(dp_count, dtype=jnp.int32)
    if paired:
        owners = jnp.bitwise_xor(owners, me)
    tile_at = jnp.logical_and(
        owner_list[None, None, :] == owners[:, None, None],
        slot[None, None, :] == jnp.arange(slot_width, dtype=jnp.int32)[None, :, None],
    )
    tile_at = jnp.sum(jnp.where(tile_at, number[None, None, :] + 1, 0), axis=2) - 1
    tile_at = tile_at.astype(jnp.int32)
    slot_here = jnp.where(owner_list == me, slot, -1)
    slot_here = slot_here.astype(jnp.int32)
    slot_number = jnp.arange(slot_width, dtype=jnp.int32)
    slot_used = jnp.sum(
        jnp.where(slot_here[None, :] == slot_number[:, None], 1, 0), axis=1
    ).astype(jnp.int32)

    full_rows = pl.BlockSpec((ROWS, model), lambda *_: (0, 0))
    small = whole((4, model))
    low_rows = shaped((ROWS, model), low_type)
    wide_rows = shaped((ROWS, model), full_type)

    scaled_rows = call(
        first_kernel,
        (1,),
        [full_rows, full_rows],
        whole((ROWS, 2 * model)),
        shaped((ROWS, 2 * model), low_type),
    )(block_in, out_grad)
    both = gather_rows(scaled_rows)
    scaled_half = pl.BlockSpec((ROWS, model), lambda s, *_: (s, 0))
    grads_half = pl.BlockSpec((tokens, model), lambda *_: (0, 1))
    image_rows = pl.BlockSpec((ROWS, model), lambda s, *_: (s, 0))

    group = slot_width // 2 if slot_width % 2 == 0 else 1
    slab = call(
        round_kernel,
        (slot_width // group,),
        [pl.BlockSpec((1, group, head, model), lambda j: (0, j, 0, 0)), any_spec],
        pl.BlockSpec((group, head, model), lambda j: (j, 0, 0)),
        shaped((slot_width, head, model), low_type),
    )(bank_w, scaled_rows)

    keys = (expert_ids * pair_count + fill_rank).astype(full_type).reshape(images, SEQ, 2)
    keys = jnp.pad(
        keys, ((0, 0), (0, ROWS - SEQ), (0, 0)), constant_values=float(2 * EXPERTS * pair_count)
    ).reshape(tokens, 2)
    router_rows = jnp.pad(router_w.astype(low_type).T, ((0, ROUTER_ROWS - EXPERTS), (0, 0)))

    half = near_tiles // 2
    half_shape = (half, head, model)

    def dispatch(keys):
        return call(
            functools.partial(dispatch_kernel, pair_count),
            (EXPERTS,),
            [whole((tokens, 2)), whole((2, tokens))],
            [
                pl.BlockSpec((1, SLOTS, tokens), lambda e: (e, 0, 0)),
                whole((tokens, EXPERTS * SLOTS)),
            ],
            [
                shaped((EXPERTS, SLOTS, tokens), low_type),
                shaped((tokens, EXPERTS * SLOTS), low_type),
            ],
            scratch=[pltpu.VMEM((2, tokens), full_type), pltpu.VMEM((tokens, 2), full_type)],
        )(keys, keys.T)

    if paired:
        near, beside = call(
            pack_kernel,
            (1,),
            [pl.BlockSpec((1, near_slots, head, model), lambda j, *_: (0, 0, 0, 0)), any_spec],
            [whole(half_shape)] * 2,
            [shaped(half_shape, low_type)] * 2,
            prefetch=2,
        )(slot_here[:near_tiles], core.reshape(1), bank_w, slab)
        pick, place = dispatch(keys)
        near = add_low(near, swap(beside))
        near = add_low(near, hop(near))
        slab_beside = after(swap(slab), [near])
        first = hop(slab)
        first_beside = hop(slab_beside)
        near = after(add_low(near, hop(near, second=True)), [both, pick])
        near_banks = [near, swap(near)]
        near_table = jnp.concatenate(
            [jnp.arange(half, dtype=jnp.int32) + lax.rem(core + i, 2) * half for i in range(2)]
        )
    else:
        pick, place = dispatch(keys)
        near_banks = [lax.all_gather(slab, "dp", axis=0, tiled=True)]
        near_table = tile_at.reshape(-1)

    width = heads * head
    all_rows = whole((tokens, model))
    all_shape = shaped((tokens, model), low_type)
    mixed_shape = (images, ROWS, 3 * width)
    attended_shape = (images, ROWS, width)
    mixed_spec = pl.BlockSpec((1,) + mixed_shape[1:], lambda s, *_: (s, 0, 0))
    attended_spec = pl.BlockSpec((1,) + attended_shape[1:], lambda s, *_: (s, 0, 0))
    normed, mixed, attended, branch = call(
        functools.partial(attend_kernel, heads, len(near_banks)),
        (images,),
        [any_spec] * len(near_banks) + [scaled_half, small, any_spec],
        [image_rows, mixed_spec, attended_spec, image_rows],
        [all_shape, shaped(mixed_shape, low_type), shaped(attended_shape, low_type), all_shape],
        scratch=[pltpu.VMEM((near_tiles, head, model), low_type), pltpu.SemaphoreType.DMA(())],
        prefetch=1,
    )(near_table, *near_banks, both, norm_w, slab)
    residual, second_rows = call(
        second_kernel,
        (1,),
        [full_rows, small, full_rows],
        [full_rows, full_rows],
        [wide_rows, low_rows],
    )(block_in, norm_w, scatter_rows(branch))
    picked_grads = call(
        pick_kernel,
        (EXPERTS,),
        [grads_half, pl.BlockSpec((1, SLOTS, tokens), lambda e: (e, 0, 0)), any_spec],
        pl.BlockSpec((1, SLOTS, model), lambda e: (e, 0, 0)),
        shaped((EXPERTS, SLOTS, model), low_type),
    )(both, pick, second_rows)
    second = gather_rows(second_rows)
    mine = jnp.where(core == 0, ALONG_X, ALONG_Y)
    other = ALONG_X + ALONG_Y - mine
    far_away = ALONG_X + ALONG_Y
    near_here = slot_here[:near_tiles]

    def plan(wanted, table):
        place = jnp.cumsum(wanted) - 1
        listed = jnp.logical_and(wanted[None, :] == 1, place[None, :] == slot_number[:, None])
        slots = jnp.sum(jnp.where(listed, slot_number[None, :], 0), axis=1).astype(jnp.int32)
        count = jnp.sum(wanted).astype(jnp.int32).reshape(1)
        return jnp.concatenate([slots, slot_used, count, table])

    if paired:

        def far_tables(*order):
            return jnp.concatenate(
                [
                    lax.dynamic_slice_in_dim(
                        slot_here, near_tiles + jnp.bitwise_xor(me, r) * runs, runs, 0
                    )
                    for r in order
                ]
            )

        def held(table):
            return jnp.sum(
                jnp.where(table[None, :] == slot_number[:, None], 1, 0), axis=1
            ).astype(jnp.int32)

        tables = [
            far_tables(0, CORE, mine, other + CORE),
            far_tables(mine + CORE, other, far_away, far_away + CORE),
            jnp.concatenate(
                [
                    lax.dynamic_slice_in_dim(near_here, lax.rem(core + i, 2) * half, half, 0)
                    for i in range(2)
                ]
            ),
        ]
        wanted = [held(table) for table in tables]
        tables.append(jnp.zeros((0,), jnp.int32))
        wanted.append(1 - slot_used)
        plans = [after(plan(w, t), [second_rows]) for w, t in zip(wanted, tables)]
    else:
        plans = []

    if paired:
        def rows_of(*order):
            return jnp.concatenate(
                [lax.dynamic_index_in_dim(tile_at, r, 0, keepdims=False) for r in order]
            )

        far_table = rows_of(0, CORE, mine, mine + CORE, other + CORE, other)
        last_table = rows_of(far_away, far_away + CORE)
        first = after(first, [first_beside])
        across = hop(first, second=True)
        far_banks = [slab, slab_beside, first, first_beside, swap(first), swap(first_beside)]
    else:
        far_banks, far_table = near_banks, near_table

    def update(table, sources, olds):
        ahead, behind = 4, 3
        return pl.pallas_call(
            functools.partial(bank_kernel, len(sources)),
            grid_spec=pltpu.PrefetchScalarGridSpec(
                num_scalar_prefetch=1,
                grid=(1,),
                in_specs=[any_spec] * (3 + len(sources) + len(olds)),
                out_specs=[any_spec] * 3,
                scratch_shapes=[
                    pltpu.VMEM((ahead, 3, head, model), full_type),
                    pltpu.VMEM((behind, 3, head, model), full_type),
                    pltpu.VMEM((slot_width, head, model), low_type),
                    pltpu.SemaphoreType.DMA((ahead, 3)),
                    pltpu.SemaphoreType.DMA((behind, 3)),
                    pltpu.SemaphoreType.DMA((slot_width,)),
                ],
            ),
            out_shape=[shaped(bank_w.shape, full_type)] * 3,
            input_output_aliases={4 + len(sources) + i: i for i in range(len(olds))},
            compiler_params=pltpu.CompilerParams(vmem_limit_bytes=VMEM_BYTES),
        )(table, bank_w, bank_m, bank_v, *sources, *olds)

    blocks = 2 * EXPERTS
    tiles_shape = (runs, head, model)
    half_blocks = (EXPERTS,) + tiles_shape
    block_number = jnp.arange(blocks, dtype=jnp.int32)
    if paired:
        order = [far_away + CORE, other, other + CORE, CORE, far_away, mine + CORE, mine, 0]
        order = jnp.bitwise_xor(me, jnp.stack([jnp.asarray(r, me.dtype) for r in order]))
        place_of = jnp.sum(
            jnp.where(order[None, :] == block_number[:, None], block_number[None, :], 0), axis=1
        )
    else:
        place_of = block_number
    expert_rows = pl.BlockSpec((1, SLOTS, model), lambda e, *_: (e, 0, 0))
    piece_shape = (ROWS + ROUTER_ROWS, model)
    pieces_shape = (images * piece_shape[0], model)
    expert_tiles = (EXPERTS, 2 * runs, head, model)

    tiles_shape_here = (far_tiles, head, model)
    tiles = call(
        functools.partial(prepare_kernel, near_tiles, len(far_banks)),
        (1,),
        [any_spec] * (len(far_banks) + 1),
        whole(tiles_shape_here),
        shaped(tiles_shape_here, low_type),
        scratch=[pltpu.SemaphoreType.DMA((far_tiles,))],
        prefetch=1,
    )(far_table, *far_banks, second_rows)
    if paired:
        across = after(across, [picked_grads, last_table, router_rows, tiles, *plans])
        across_swapped = region(flag, swap, across)
        tiles = pl.pallas_call(
            functools.partial(place_kernel, near_tiles, 2),
            grid_spec=pltpu.PrefetchScalarGridSpec(
                num_scalar_prefetch=1,
                grid=(1,),
                in_specs=[any_spec] * 3,
                out_specs=any_spec,
                scratch_shapes=[
                    pltpu.VMEM(tiles_shape_here, low_type),
                    pltpu.SemaphoreType.DMA((far_tiles,)),
                    pltpu.SemaphoreType.DMA((far_tiles,)),
                ],
            ),
            out_shape=shaped(tiles_shape_here, low_type),
            input_output_aliases={3: 0},
            compiler_params=pltpu.CompilerParams(vmem_limit_bytes=VMEM_BYTES),
        )(last_table, across, across_swapped, tiles)
    sent_first, sent, kept, gated, pieces = call(
        functools.partial(expert_kernel, images, runs),
        (EXPERTS,),
        [
            pl.BlockSpec((1,) + expert_tiles[1:], lambda e, *_: (e, 0, 0, 0)),
            expert_rows,
            all_rows,
            whole((ROUTER_ROWS, model)),
            pl.BlockSpec((1, SLOTS, tokens), lambda e, *_: (e, 0, 0)),
            any_spec,
        ],
        [any_spec, any_spec, any_spec, expert_rows, whole(pieces_shape)],
        [
            shaped(tiles_shape, low_type),
            shaped((EXPERTS - 1,) + tiles_shape, low_type),
            shaped(half_blocks, low_type),
        ]
        + [shaped((EXPERTS, SLOTS, model), low_type), shaped(pieces_shape, low_type)],
        scratch=[
            pltpu.VMEM((ROUTER_ROWS, tokens), full_type),
            pltpu.VMEM((ROUTER_ROWS, tokens), full_type),
            pltpu.VMEM((EXPERTS * SLOTS, model), low_type),
            pltpu.VMEM((tokens, EXPERTS * SLOTS), low_type),
            pltpu.VMEM((2, 2) + tiles_shape, low_type),
            pltpu.SemaphoreType.DMA((2, 2)),
            pltpu.SemaphoreType.DMA(()),
        ],
        prefetch=1,
    )(
        place_of.astype(jnp.int32),
        tiles.reshape(expert_tiles),
        picked_grads,
        second,
        router_rows,
        pick,
        place,
    )
    piece = scatter_rows(pieces)

    def combine(gated):
        return call(
            combine_kernel,
            (images,),
            [
                whole((EXPERTS * SLOTS, model)),
                pl.BlockSpec((ROWS, EXPERTS * SLOTS), lambda s: (s, 0)),
            ],
            image_rows,
            all_shape,
        )(gated.reshape(EXPERTS * SLOTS, model), place)

    def sum_far(sent_first, sent, kept, gated):
        across = add_low(kept[0], swap(sent_first))
        part = swap(after(sent, [across]))
        across = hop(across, second=True)
        combined = combine(gated)
        beside = hop(add_low(kept[1], part[0]))
        return combined, part, beside, add_low(kept[2], part[1], across)

    if paired:
        combined, part, beside, along = region(flag, sum_far, sent_first, sent, kept, gated)
        ordered = [along]
    else:
        combined, ordered = combine(gated), []

    residual_grad, branch_rows, small_two = call(
        second_back_kernel,
        (1,),
        [full_rows, full_rows, full_rows, whole((ROUTER_ROWS, model)), small, whole(piece_shape)]
        + [any_spec] * len(ordered),
        [full_rows, full_rows, whole((8, model))],
        [wide_rows, low_rows, shaped((8, model), full_type)],
    )(residual, out_grad, second_rows, router_rows, norm_w, piece, *ordered)
    branch_grads = gather_rows(branch_rows)

    if paired:

        def sum_own(kept, part, beside, along, plan):
            own = add_low(kept[3], part[2], hop(along), swap(beside))
            return update(plan, [], []), own, swap(own), hop(own)

        own_blocks = region(
            flag, sum_own, kept, part, beside, after(along, [branch_rows]), plans[3]
        )
    else:
        products = jnp.concatenate([sent_first[None], sent, kept], axis=0)
        products = products.reshape(far_tiles, head, model)
        far_sources = [total_tiles(products)]
        far_slots_here = [
            jnp.pad(
                slot_here[near_tiles:],
                (0, far_sources[0].shape[0] - far_tiles),
                constant_values=-1,
            )
        ]

    here = lax.axis_index("tensor").astype(jnp.int32).reshape(1)
    near_rows = half * head
    near_shape = (near_rows + 16, model)
    def add_near(left, right, before=(), apart=False):
        shapes = [(near_rows, model), (16, model)] if apart else [near_shape]
        out = call(
            functools.partial(near_add_kernel, len(shapes)),
            (1,),
            [whole(near_shape)] * 2 + [any_spec] * len(before),
            [whole(shape) for shape in shapes],
            [shaped(shape, low_type) for shape in shapes],
        )(left, right, *before)
        return out if apart else out[0]

    def attend_back(branch_grads, small_two):
        return call(
            functools.partial(attend_back_kernel, images, heads, len(near_banks)),
            (images,),
            [any_spec] * len(near_banks)
            + [image_rows, scaled_half, image_rows, mixed_spec, attended_spec]
            + [whole((8, model))],
            [whole(near_shape)] * 2 + [image_rows, whole((8, model))],
            [shaped(near_shape, low_type)] * 2 + [all_shape, shaped((8, model), full_type)],
            scratch=[
                pltpu.VMEM((near_tiles, head, model), low_type),
                pltpu.VMEM((tokens, model), low_type),
                pltpu.VMEM((tokens, model), low_type),
                pltpu.VMEM((tokens, 3 * width), low_type),
                pltpu.VMEM((tokens, width), low_type),
                pltpu.SemaphoreType.DMA(()),
            ],
            prefetch=2,
        )(
            near_table,
            core.reshape(1),
            *near_banks,
            branch_grads,
            both,
            normed,
            mixed,
            attended,
            small_two,
        )

    def third(branch_grads, small_two, plan, banks, own, own_beside, first):
        far = [hop(own_beside), hop(first, second=True)]
        early = [own, own_beside, first, swap(first)]
        near, beside, pieces, _ = attend_back(branch_grads, small_two)
        near = add_near(near, swap(beside))
        return near, pieces, far, update(plan, early, banks)

    combined = scatter_rows(combined)
    if paired:
        near, pieces, far, banks = region(
            flag, third, branch_grads, small_two, plans[0], *own_blocks
        )
        pieces = after(pieces, [combined])
    else:
        near_own, near_beside, pieces, sums = attend_back(branch_grads, small_two)
    pieces = scatter_rows(pieces)

    def finish(far, own, banks, plans):
        late = [p for block in far for p in (block, swap(block))]
        banks = update(plans[0], late, banks)
        own, sums = add_near(own, hop(own), banks[:1], apart=True)
        sums = [sums] + collect_rows(sums)
        sums = call(
            functools.partial(last_sum_kernel, images),
            (1,),
            [whole((16, model))] * images,
            whole((8, model)),
            shaped((8, model), full_type),
            scratch=[pltpu.VMEM((images, 8, model), full_type)],
            prefetch=1,
        )(here, *sums)
        own = add_low(own, after(hop(own, second=True), [sums]))
        tiles_here = own.reshape(half_shape)
        other_sums = hop(sums, second=True)
        banks = update(plans[1], [tiles_here, swap(tiles_here)], banks)
        sums = sums + after(other_sums, [banks[2]])
        return *banks, sums

    if paired:
        bank_first, bank_second, bank_new, sums = region(
            flag, finish, far, near, banks, plans[1:3]
        )
    else:
        near_grads = jnp.concatenate([near_own[:near_rows], near_beside[:near_rows]], axis=0)
        near_sources = [total_tiles(near_grads.reshape(near_tiles, head, model))]
        near_slots_here = [
            jnp.pad(near_here, (0, near_sources[0].shape[0] - near_tiles), constant_values=-1)
        ]
        sums = butterfly(butterfly(sums, "tensor"), "dp")
        table = jnp.concatenate([far_slots_here[0], near_slots_here[0]])
        bank_first, bank_second, bank_new = update(
            plan(jnp.ones((slot_width,), jnp.int32), table), far_sources + near_sources, []
        )
    input_grad, block_out = call(
        first_back_kernel,
        (1,),
        [full_rows, full_rows, small, full_rows, full_rows, full_rows, any_spec],
        [full_rows, full_rows],
        [shaped((SEQ, model), full_type)] * 2,
    )(block_in, residual_grad, norm_w, residual, pieces, combined, bank_new)
    norm_grad = sums[:4]
    router_total = sums[4:].T
    norm_first, norm_second, norm_new = adamw_update(
        norm_w, norm_m, norm_v, norm_grad, rate_norm, 0.0
    )
    router_first, router_second, router_new = adamw_update(
        router_w, router_m, router_v, router_total, rate_router, weight_decay
    )
    return (
        block_out,
        input_grad,
        bank_first,
        bank_second,
        bank_new,
        norm_first,
        norm_second,
        norm_new,
        router_first,
        router_second,
        router_new,
    )


def solution(mesh):
    rows = P(("dp", "tensor"), None)
    bank = P("tensor", "dp", None, None)
    return jax.shard_map(
        on_device,
        mesh=mesh,
        in_specs=(rows, rows, bank, bank, bank) + (P(),) * 6 + (P("dp", None), P("dp", None), P()),
        out_specs=(rows, rows, bank, bank, bank) + (P(),) * 6,
        check_vma=False,
    )
```
